32 devices in a mesh: segment: 4 (over x, core), strip: 8 (over z, y).
Axes of the slice: x: 2, y: 2, z: 4, core: 2. Of those that a mesh axis runs over, the one named last changes fastest.
Arguments:
- features: bfloat16 [2, 256, 128, 256], P(None, 'segment', 'strip'), may hold values from -6 to 6
- weight_first: bfloat16 [3, 3, 256, 256], replicated, may hold values from -0.125 to 0.125
- weight_second: bfloat16 [3, 3, 256, 256], replicated, may hold values from -0.125 to 0.125
- weight_down: bfloat16 [2, 2, 256, 512], replicated, may hold values from -0.1875 to 0.1875
- section_weights: bfloat16 [4, 3, 3, 512, 512], P('segment'), may hold values from -0.09375 to 0.09375
Outputs:
- section_features: bfloat16 [4, 2, 128, 64, 512], P('segment', None, 'strip')
The draws below stay inside these ranges and needn't reach their ends.
All inputs are finite; a program needn't handle non-finite values.
Results may differ from the reference program's by a relative error of at most 0.0095.
Values may be sent and summed in bfloat16 or wider, within the bound.
A program may use at most 128 MiB of HBM per device.

```python
import jax
import jax.numpy as jnp

C1 = 256
C2 = 512
WINDOWS = 2
SECTIONS = 4
H = 256
W = 128


def level_of(rng, shape, pieces, smallest, high):
    def one(axis_at, shards_of):
        draws = jax.random.uniform(jax.random.fold_in(jax.random.fold_in(rng, 6), axis_at), (shards_of,), jnp.float32, smallest / len(pieces), high / len(pieces))
        return jnp.repeat(jnp.exp(draws), shape[axis_at] // shards_of).reshape((-1,) + (1,) * (len(shape) - axis_at - 1))

    gain = one(*pieces[0])
    for cut in pieces[1:]:
        gain = gain * one(*cut)
    return gain


def bell_draw(rng, extent, scale, bound, shards=(), dtype=jnp.bfloat16):
    entries = scale * jax.random.normal(rng, extent, jnp.float32)
    if shards:
        entries = entries * level_of(rng, extent, shards, -0.22, 0.18)
    return jnp.clip(entries, -bound, bound).astype(dtype)


def setup_inputs(seed: int = 0) -> dict:
    key_list = jax.random.split(jax.random.key(seed), 6)
    features = bell_draw(key_list[0], (WINDOWS, H, W, C1), 1.0, 6.0, ((1, 4), (2, 8)))
    weight_first = bell_draw(key_list[1], (3, 3, C1, C1), (9 * C1) ** -0.5, 0.125)
    weight_second = bell_draw(key_list[2], (3, 3, C1, C1), (9 * C1) ** -0.5, 0.125)
    weight_down = bell_draw(key_list[3], (2, 2, C1, C2), (4 * C1) ** -0.5, 0.1875)
    section_weights = bell_draw(key_list[4], (SECTIONS, 3, 3, C2, C2), (9 * C2) ** -0.5, 0.09375, ((0, 4),))
    return dict(features=features, weight_first=weight_first, weight_second=weight_second, weight_down=weight_down, section_weights=section_weights)


def conv_valid(padded, weight):
    batches, rows_pad, columns_pad, channels = padded.shape
    rows = rows_pad - 2
    columns = columns_pad - 2
    total = None
    for row_off in range(3):
        for col_off in range(3):
            window = padded[:, row_off:row_off + rows, col_off:col_off + columns, :].reshape(-1, channels)
            partial_sum = jnp.dot(window, weight[row_off, col_off], preferred_element_type=jnp.float32)
            total = partial_sum if total is None else total + partial_sum
    return total.reshape(batches, rows, columns, weight.shape[3])


def residual_layer(inputs, weight):
    padded = jnp.pad(inputs, ((0, 0), (1, 1), (1, 1), (0, 0)))
    return jax.nn.relu(inputs.astype(jnp.float32) + conv_valid(padded, weight)).astype(jnp.bfloat16)


def reference(features, weight_first, weight_second, weight_down, section_weights):
    first = residual_layer(features, weight_first)
    second = residual_layer(first, weight_second)
    batches, rows, columns, channels = second.shape
    blocks = second.reshape(batches, rows // 2, 2, columns // 2, 2, channels)
    total = None
    for row_off in range(2):
        for col_off in range(2):
            piece = blocks[:, :, row_off, :, col_off, :].reshape(-1, channels)
            partial_sum = jnp.dot(piece, weight_down[row_off, col_off], preferred_element_type=jnp.float32)
            total = partial_sum if total is None else total + partial_sum
    current = jax.nn.relu(total).reshape(batches, rows // 2, columns // 2, weight_down.shape[3]).astype(jnp.bfloat16)
    stacked = []
    for section in range(SECTIONS):
        current = residual_layer(current, section_weights[section])
        stacked.append(current)
    return jnp.stack(stacked)
```

```python
import functools

import jax
import jax.numpy as jnp
import numpy as np
from jax import lax
from jax.experimental import pallas as pl
from jax.experimental.pallas import tpu as pltpu
from jax.sharding import PartitionSpec as P

MESH = pl.DeviceIdType.MESH
EDGE = 16
DIRS = [(dg, ds) for dg in (-1, 0, 1) for ds in (-1, 0, 1) if (dg, ds) != (0, 0)]


def fits(count, pitch, limit):
    best = 1
    for size in range(1, count + 1):
        if count % size == 0 and size * pitch <= limit:
            best = size
    return best


def kernel(
    dims,
    feat,
    wf,
    ws,
    wd,
    wsec,
    perm,
    out,
    x_buf,
    f_buf,
    s_buf,
    d_buf,
    r_buf,
    z_buf,
    o_buf,
    wf_v,
    ws_v,
    wd_v,
    wsec_v,
    wsem,
    fsem,
    hsend,
    hrecv,
    rsend,
    rmain,
    rtop,
    rbot,
    csend,
    crecv,
    esend,
    erecv,
    osem,
):
    S, N, B, R, C, K1, K2 = dims
    RD, CD = R // 2, C // 2
    m = N // S
    sr = RD // m
    cols = CD * N
    cr = max(1, 256 // cols)
    n = sr // cr
    pitch = R + 2 * EDGE
    g = lax.axis_index("segment")
    s = lax.axis_index("strip")

    copies = []
    for a in range(3):
        for c in range(3):
            copies.append(
                (0, wf.at[a, c], wf_v.at[pl.ds(c * K1, K1), pl.ds(a * K1, K1)])
            )
    for a in range(3):
        for c in range(3):
            copies.append(
                (1, ws.at[a, c], ws_v.at[pl.ds(c * K1, K1), pl.ds(a * K1, K1)])
            )
    for a in range(2):
        for c in range(2):
            copies.append((2, wd.at[a, c], wd_v.at[pl.ds((2 * a + c) * K1, K1)]))
    for a in range(3):
        for c in range(3):
            copies.append(
                (3, wsec.at[0, a, c], wsec_v.at[pl.ds(a * K2, K2), pl.ds(c * K2, K2)])
            )
    weights = [
        (group, pltpu.make_async_copy(src, dst, wsem.at[i]))
        for i, (group, src, dst) in enumerate(copies)
    ]

    def weights_wait(which):
        for group, copy in weights:
            if group == which:
                copy.wait()

    centre = [
        pltpu.make_async_copy(
            feat.at[b], x_buf.at[b, pl.ds(2, C), pl.ds(EDGE, R)], fsem.at[b]
        )
        for b in range(B)
    ]
    for copy in centre:
        copy.start()
    for _, copy in weights:
        copy.start()

    zero = jnp.bfloat16(0)
    x_buf[:, 0:2] = jnp.full((B, 2, pitch, K1), zero)
    x_buf[:, C + 2 : C + 4] = jnp.full((B, 2, pitch, K1), zero)
    x_buf[:, 2 : C + 2, 0:EDGE] = jnp.full((B, C, EDGE, K1), zero)
    x_buf[:, 2 : C + 2, EDGE + R :] = jnp.full((B, C, EDGE, K1), zero)
    z_buf[:, 0] = jnp.full((B, cols, K2), zero)
    z_buf[:, sr + 1] = jnp.full((B, cols, K2), zero)
    r_buf[:, :, 0 : 2 * CD] = jnp.full((B, N, 2 * CD, K2), zero)
    r_buf[:, :, (sr + 2) * CD :] = jnp.full((B, N, 2 * CD, K2), zero)

    barrier = pltpu.get_barrier_semaphore()
    total = S * N
    me = g * N + s

    def greet(k, carry):
        other = lax.rem(me + k, total)
        pl.semaphore_signal(
            barrier,
            inc=1,
            device_id=(lax.div(other, N), lax.rem(other, N)),
            device_id_type=MESH,
        )
        return carry

    lax.fori_loop(1, total, greet, 0)
    pl.semaphore_wait(barrier, total - 1)

    def inside(gg, ss):
        return (gg >= 0) & (gg < S) & (ss >= 0) & (ss < N)

    row_src = {-1: (0, EDGE), 0: (0, R), 1: (R - EDGE, EDGE)}
    row_dst = {-1: EDGE + R, 0: EDGE, 1: 0}
    col_src = {-1: (0, 2), 0: (0, C), 1: (C - 2, 2)}
    col_dst = {-1: C + 2, 0: 2, 1: 0}

    def border(b, i):
        dg, ds = DIRS[i]
        r0, rn = row_src[dg]
        c0, cn = col_src[ds]
        return pltpu.make_async_remote_copy(
            src_ref=feat.at[b, pl.ds(c0, cn), pl.ds(r0, rn)],
            dst_ref=x_buf.at[b, pl.ds(col_dst[ds], cn), pl.ds(row_dst[dg], rn)],
            send_sem=hsend.at[b, i],
            recv_sem=hrecv.at[b, i],
            device_id=(g + dg, s + ds),
            device_id_type=MESH,
        )

    for b in range(B):
        for i, (dg, ds) in enumerate(DIRS):

            @pl.when(inside(g + dg, s + ds))
            def _():
                border(b, i).start()

    def pieces(b):
        found = []
        for k in range(m):
            low, high = max(0, k * sr - 2), min(RD, k * sr + sr + 2)
            found.append(
                (
                    g * m + k,
                    True,
                    low,
                    high - low,
                    low - (k * sr - 2),
                    rmain,
                )
            )
        found.append((g * m - 1, g > 0, 0, 2, sr + 2, rbot))
        found.append((g * m + m, g < S - 1, RD - 2, 2, 0, rtop))
        made = []
        for i, (strip, active, low, count, at, sem) in enumerate(found):
            src = d_buf.at[b, pl.ds(low * CD, count * CD)]
            dst = r_buf.at[b, s, pl.ds(at * CD, count * CD)]
            remote = functools.partial(
                pltpu.make_async_remote_copy,
                src_ref=src,
                dst_ref=dst,
                send_sem=rsend.at[b, i],
                recv_sem=sem.at[b, s],
                device_id=(0, strip),
                device_id_type=MESH,
            )
            local = functools.partial(pltpu.make_async_copy, src, dst, sem.at[b, s])
            own = (g == 0) & (s == strip)
            made.append((active & ~own, active & own, remote, local))
        return made

    def conv_rows(buf, first_col, size, weight, sel):
        data = [
            buf[sel(first_col + j, size)].reshape(size * pitch, K1) for j in range(3)
        ]
        data = jnp.concatenate(data, axis=1)
        part = [
            jnp.dot(
                data,
                weight[:, a * K1 : (a + 1) * K1],
                preferred_element_type=jnp.float32,
            )
            for a in range(3)
        ]
        rows = size * pitch
        return pltpu.roll(part[0], 1, 0) + part[1] + pltpu.roll(part[2], rows - 1, 0)

    size1 = fits(C + 2, pitch, 320)
    size2 = fits(C, pitch, 400)

    def stem(b):
        centre[b].wait()
        for i, (dg, ds) in enumerate(DIRS):

            @pl.when(inside(g - dg, s - ds))
            def _():
                border(b, i).wait_recv()

        if b == 0:
            weights_wait(0)

        def one(t, carry):
            c0 = t * size1
            conv = conv_rows(
                x_buf, c0, size1, wf_v, lambda at, size: (b, pl.ds(at, size))
            )
            conv = conv.reshape(size1, pitch, K1)
            inner = x_buf[b, pl.ds(c0 + 1, size1)].astype(jnp.float32)
            value = jnp.maximum(inner + conv, 0.0)
            col = lax.broadcasted_iota(jnp.int32, (size1, pitch, K1), 0) + (
                s * C + c0 - 1
            )
            row = lax.broadcasted_iota(jnp.int32, (size1, pitch, K1), 1) + (g * R - EDGE)
            keep = (col >= 0) & (col < N * C) & (row >= 0) & (row < S * R)
            f_buf[pl.ds(c0, size1)] = jnp.where(keep, value, 0.0).astype(jnp.bfloat16)
            return carry

        lax.fori_loop(0, (C + 2) // size1, one, 0)
        if b == 0:
            weights_wait(1)

        def two(t, carry):
            c0 = t * size2
            conv = conv_rows(f_buf, c0, size2, ws_v, lambda at, size: (pl.ds(at, size),))
            conv = conv.reshape(size2, pitch, K1)[:, EDGE : EDGE + R]
            inner = f_buf[pl.ds(c0 + 1, size2), EDGE : EDGE + R].astype(jnp.float32)
            value = jnp.maximum(inner + conv, 0.0)
            at = pl.multiple_of(c0 * R, R)
            value = value.reshape(size2 * R, K1)
            for q in range(K1 // 128):
                s_buf[q, pl.ds(at, size2 * R), :] = value[:, q * 128 : (q + 1) * 128]
            return carry

        lax.fori_loop(0, C // size2, two, 0)
        if b == 0:
            weights_wait(2)
        taps = []
        for a in range(2):
            picked = jnp.concatenate(
                [
                    s_buf[q, pl.ds(a, C * RD, stride=2), :]
                    for q in range(K1 // 128)
                ],
                axis=1,
            )
            picked = picked.reshape(CD, 2, RD, K1)
            for c in range(2):
                taps.append(picked[:, c].reshape(CD * RD, K1).astype(jnp.bfloat16))
        reduced = jnp.dot(
            jnp.concatenate(taps, axis=1), wd_v[...], preferred_element_type=jnp.float32
        )
        reduced = jnp.maximum(reduced, 0.0).astype(jnp.bfloat16)
        d_buf[b] = jnp.dot(
            perm[...], reduced, preferred_element_type=jnp.float32
        ).astype(jnp.bfloat16)
        for away, home, remote, local in pieces(b):

            @pl.when(away)
            def _():
                remote().start()

            @pl.when(home)
            def _():
                local().start()

    for b in range(B):
        stem(b)
    weights_wait(3)

    def arrive(b):
        def waits(src, carry):
            for k in range(m):
                low, high = max(0, k * sr - 2), min(RD, k * sr + sr + 2)
                part = r_buf.at[
                    b, src, pl.ds((low - (k * sr - 2)) * CD, (high - low) * CD)
                ]

                @pl.when(lax.rem(s, m) == k)
                def _():
                    pltpu.make_async_copy(part, part, rmain.at[b, src]).wait()

            top = r_buf.at[b, src, pl.ds(0, 2 * CD)]
            bottom = r_buf.at[b, src, pl.ds((sr + 2) * CD, 2 * CD)]

            @pl.when((lax.rem(s, m) == 0) & (s > 0))
            def _():
                pltpu.make_async_copy(top, top, rtop.at[b, src]).wait()

            @pl.when((lax.rem(s, m) == m - 1) & (s < N - 1))
            def _():
                pltpu.make_async_copy(bottom, bottom, rbot.at[b, src]).wait()

            return carry

        lax.fori_loop(0, N, waits, 0)
        group = max(1, EDGE // CD)
        for q in range(N // group):
            parts = [
                r_buf[b, q * group + j]
                .astype(jnp.float32)
                .reshape(sr + 4, CD, K2)[1 : sr + 3]
                for j in range(group)
            ]
            whole = parts[0] if group == 1 else jnp.concatenate(parts, axis=1)
            z_buf[b, :, q * group * CD : (q + 1) * group * CD] = whole.astype(
                jnp.bfloat16
            )

    def chunk_copy(b, k):
        rows = pl.ds(k * cr, cr)
        return pltpu.make_async_remote_copy(
            src_ref=o_buf.at[b, rows],
            dst_ref=z_buf.at[b, pl.ds(k * cr + 1, cr)],
            send_sem=csend.at[b, k],
            recv_sem=crecv.at[b, k],
            device_id=(g + 1, s),
            device_id_type=MESH,
        )

    def edge_copy(b, low):
        src, dst, to = (0, sr + 1, s - 1) if low else (sr - 1, 0, s + 1)
        i = 0 if low else 1
        return pltpu.make_async_remote_copy(
            src_ref=o_buf.at[b, pl.ds(src, 1)],
            dst_ref=z_buf.at[b, pl.ds(dst, 1)],
            send_sem=esend.at[b, i],
            recv_sem=erecv.at[b, i],
            device_id=(g + 1, to),
            device_id_type=MESH,
        )

    def out_copy(b, k):
        rows = pl.ds(k * cr, cr)
        return pltpu.make_async_copy(
            o_buf.at[b, rows], out.at[0, b, rows], osem.at[b, k]
        )

    span = cr * cols
    width = 256

    def section(b, p):
        k = jnp.where(p == n - 1, n - 1, jnp.where(p == n - 2, 0, p + 1))

        @pl.when(g > 0)
        def _():
            @pl.when(p == 0)
            def _():
                for j in range(3):
                    chunk_copy(b, j).wait_recv()

            @pl.when((p > 0) & (p < n - 2))
            def _():
                chunk_copy(b, p + 2).wait_recv()

            @pl.when((p == n - 2) & (s > 0))
            def _():
                edge_copy(b, False).wait_recv()

            @pl.when((p == n - 1) & (s < N - 1))
            def _():
                edge_copy(b, True).wait_recv()

        data = jnp.concatenate(
            [z_buf[b, pl.ds(k * cr + a, cr)].reshape(span, K2) for a in range(3)],
            axis=1,
        )
        place = lax.broadcasted_iota(jnp.int32, (cr, cols, width), 1).reshape(span, width)
        for q in range(K2 // width):
            part = [
                jnp.dot(
                    data,
                    wsec_v[:, c * K2 + q * width : c * K2 + (q + 1) * width],
                    preferred_element_type=jnp.float32,
                )
                for c in range(3)
            ]
            left = jnp.where(place == 0, 0.0, pltpu.roll(part[0], 1, 0))
            right = jnp.where(place == cols - 1, 0.0, pltpu.roll(part[2], span - 1, 0))
            inner = z_buf[
                b, pl.ds(k * cr + 1, cr), :, q * width : (q + 1) * width
            ].reshape(span, width)
            value = jnp.maximum(inner.astype(jnp.float32) + left + part[1] + right, 0.0)
            o_buf[b, pl.ds(k * cr, cr), :, q * width : (q + 1) * width] = value.astype(
                jnp.bfloat16
            ).reshape(cr, cols, width)
        out_copy(b, k).start()

        @pl.when(g < S - 1)
        def _():
            @pl.when((k == 0) & (s > 0))
            def _():
                edge_copy(b, True).start()

            @pl.when((k == n - 1) & (s < N - 1))
            def _():
                edge_copy(b, False).start()

            chunk_copy(b, k).start()

    for b in range(B):

        @pl.when(g == 0)
        def _():
            arrive(b)

        def step(p, carry):
            section(b, p)
            return carry

        lax.fori_loop(0, n, step, 0)

    for b in range(B):
        for i, (dg, ds) in enumerate(DIRS):

            @pl.when(inside(g + dg, s + ds))
            def _():
                border(b, i).wait_send()

        for away, home, remote, local in pieces(b):

            @pl.when(away)
            def _():
                remote().wait_send()

        @pl.when(g < S - 1)
        def _():
            @pl.when(s > 0)
            def _():
                edge_copy(b, True).wait_send()

            @pl.when(s < N - 1)
            def _():
                edge_copy(b, False).wait_send()

            for k in range(n):
                chunk_copy(b, k).wait_send()

        for k in range(n):
            out_copy(b, k).wait()


def shards(S, N, features, weight_first, weight_second, weight_down, section_weights):
    B, R, C, K1 = features.shape
    K2 = weight_down.shape[3]
    RD, CD = R // 2, C // 2
    m = N // S
    sr = RD // m
    cols = CD * N
    n = sr // max(1, 256 // cols)
    pitch = R + 2 * EDGE
    p = np.arange(RD * CD)
    perm = (np.arange(RD * CD)[None, :] == ((p % CD) * RD + p // CD)[:, None])
    perm = jnp.asarray(perm, jnp.bfloat16)
    bf16, f32 = jnp.bfloat16, jnp.float32
    dma = pltpu.SemaphoreType.DMA
    anywhere = pl.BlockSpec(memory_space=pl.ANY)
    flops = 2 * B * (R * C * 18 * K1 * K1 + RD * CD * 4 * K1 * K2 + sr * cols * 9 * K2 * K2)
    return pl.pallas_call(
        functools.partial(kernel, (S, N, B, R, C, K1, K2)),
        out_shape=jax.ShapeDtypeStruct((1, B, sr, cols, K2), bf16),
        in_specs=[anywhere] * 5 + [pl.BlockSpec(memory_space=pltpu.VMEM)],
        out_specs=anywhere,
        scratch_shapes=[
            pltpu.VMEM((B, C + 4, pitch, K1), bf16),
            pltpu.VMEM((C + 2, pitch, K1), bf16),
            pltpu.VMEM((K1 // 128, C * R, 128), f32),
            pltpu.VMEM((B, RD * CD, K2), bf16),
            pltpu.VMEM((B, N, (sr + 4) * CD, K2), bf16),
            pltpu.VMEM((B, sr + 2, cols, K2), bf16),
            pltpu.VMEM((B, sr, cols, K2), bf16),
            pltpu.VMEM((3 * K1, 3 * K1), bf16),
            pltpu.VMEM((3 * K1, 3 * K1), bf16),
            pltpu.VMEM((4 * K1, K2), bf16),
            pltpu.VMEM((3 * K2, 3 * K2), bf16),
            dma((31,)),
            dma((B,)),
            dma((B, 8)),
            dma((B, 8)),
            dma((B, m + 2)),
            dma((B, N)),
            dma((B, N)),
            dma((B, N)),
            dma((B, n)),
            dma((B, n)),
            dma((B, 2)),
            dma((B, 2)),
            dma((B, n)),
        ],
        compiler_params=pltpu.CompilerParams(
            collective_id=0, has_side_effects=True, vmem_limit_bytes=56 * 1024 * 1024
        ),
        cost_estimate=pl.CostEstimate(
            flops=flops, bytes_accessed=16 * 1024 * 1024, transcendentals=0
        ),
    )(
        jnp.transpose(features, (0, 2, 1, 3)),
        weight_first,
        weight_second,
        weight_down,
        section_weights,
        perm,
    )


def solution(mesh):
    return jax.shard_map(
        functools.partial(shards, mesh.shape["segment"], mesh.shape["strip"]),
        mesh=mesh,
        in_specs=(
            P(None, "segment", "strip", None),
            P(),
            P(),
            P(),
            P("segment", None, None, None, None),
        ),
        out_specs=P("segment", None, "strip", None, None),
        check_vma=False,
    )
```

```python
import functools

import jax
import jax.numpy as jnp
from jax import lax
from jax.experimental import pallas as pl
from jax.experimental.pallas import tpu as pltpu
from jax.sharding import PartitionSpec as P

MESH = pl.DeviceIdType.MESH
EDGE = 16
DIRS = [(dg, ds) for dg in (-1, 0, 1) for ds in (-1, 0, 1) if (dg, ds) != (0, 0)]


def fits(count, pitch, limit):
    best = 1
    for size in range(1, count + 1):
        if count % size == 0 and size * pitch <= limit:
            best = size
    return best


def kernel(
    dims,
    feat,
    wf,
    ws,
    wd,
    wsec,
    out,
    raw_buf,
    top_buf,
    bot_buf,
    x_buf,
    f_buf,
    s_buf,
    d_buf,
    r_buf,
    z_buf,
    o_buf,
    wf_v,
    ws_v,
    wd_v,
    wsec_v,
    wsem,
    fsem,
    hsend,
    hrecv,
    rsend,
    rmain,
    csend,
    crecv,
    zsend,
    esend,
    erecv,
    osem,
):
    S, N, B, R, C, K1, K2 = dims
    RD, CD = R // 2, C // 2
    m = N // S
    sr = RD // m
    cols = CD * N
    cr = max(1, 256 // cols)
    n = sr // cr
    pitch = R + EDGE
    g = lax.axis_index("segment")
    s = lax.axis_index("strip")

    copies = []
    for a in range(3):
        for c in range(3):
            copies.append(
                (0, wf.at[a, c], wf_v.at[pl.ds(c * K1, K1), pl.ds(a * K1, K1)])
            )
    for a in range(3):
        for c in range(3):
            copies.append(
                (1, ws.at[a, c], ws_v.at[pl.ds(c * K1, K1), pl.ds(a * K1, K1)])
            )
    for a in range(2):
        for c in range(2):
            copies.append((2, wd.at[a, c], wd_v.at[pl.ds((2 * a + c) * K1, K1)]))
    for a in range(3):
        for c in range(3):
            copies.append(
                (3, wsec.at[0, a, c], wsec_v.at[pl.ds(a * K2, K2), pl.ds(c * K2, K2)])
            )
    weights = [
        (group, pltpu.make_async_copy(src, dst, wsem.at[i]))
        for i, (group, src, dst) in enumerate(copies)
    ]

    def weights_wait(which):
        for group, copy in weights:
            if group == which:
                copy.wait()

    centre = [
        pltpu.make_async_copy(
            feat.at[b], raw_buf.at[b], fsem.at[b]
        )
        for b in range(B)
    ]
    for copy in centre:
        copy.start()
    for _, copy in weights:
        copy.start()

    zero = jnp.bfloat16(0)
    x_buf[:, 0:2] = jnp.full((B, 2, pitch, K1), zero)
    x_buf[:, C + 2 : C + 4] = jnp.full((B, 2, pitch, K1), zero)
    top_buf[...] = jnp.full((B, C + 4, EDGE, K1), zero)
    bot_buf[...] = jnp.full((B, C + 4, EDGE, K1), zero)
    z_buf[:, 0] = jnp.full((B, cols, K2), zero)
    z_buf[:, sr + 1] = jnp.full((B, cols, K2), zero)

    def swap(outer, inner):
        shape = (inner, outer, outer * inner)
        i, j, q = [lax.broadcasted_iota(jnp.int32, shape, d) for d in range(3)]
        hot = jnp.where(q == j * inner + i, 1.0, 0.0)
        return hot.reshape(outer * inner, outer * inner).astype(jnp.bfloat16)

    turn = swap(EDGE, C)
    for b in range(B):
        centre[b].wait()
        for q in range(R // EDGE):
            block = raw_buf[b, q * EDGE : (q + 1) * EDGE].reshape(EDGE * C, K1)
            block = jnp.dot(turn, block, preferred_element_type=jnp.float32)
            x_buf[b, 2 : C + 2, q * EDGE : (q + 1) * EDGE] = block.astype(
                jnp.bfloat16
            ).reshape(C, EDGE, K1)

    barrier = pltpu.get_barrier_semaphore()
    total = S * N
    me = g * N + s

    def greet(k, carry):
        other = lax.rem(me + k, total)
        pl.semaphore_signal(
            barrier,
            inc=1,
            device_id=(lax.div(other, N), lax.rem(other, N)),
            device_id_type=MESH,
        )
        return carry

    lax.fori_loop(1, total, greet, 0)
    pl.semaphore_wait(barrier, total - 1)

    def inside(gg, ss):
        return (gg >= 0) & (gg < S) & (ss >= 0) & (ss < N)

    row_src = {-1: (0, EDGE), 0: (0, R), 1: (R - EDGE, EDGE)}
    col_src = {-1: (2, 2), 0: (2, C), 1: (C, 2)}
    col_dst = {-1: C + 2, 0: 2, 1: 0}

    def border(b, i):
        dg, ds = DIRS[i]
        r0, rn = row_src[dg]
        c0, cn = col_src[ds]
        where = pl.ds(col_dst[ds], cn)
        if dg == 0:
            dst = x_buf.at[b, where, pl.ds(0, R)]
        else:
            dst = (top_buf if dg == 1 else bot_buf).at[b, where]
        return pltpu.make_async_remote_copy(
            src_ref=x_buf.at[b, pl.ds(c0, cn), pl.ds(r0, rn)],
            dst_ref=dst,
            send_sem=hsend.at[b, i],
            recv_sem=hrecv.at[b, i],
            device_id=(g + dg, s + ds),
            device_id_type=MESH,
        )

    for b in range(B):
        for i, (dg, ds) in enumerate(DIRS):

            @pl.when(inside(g + dg, s + ds))
            def _():
                border(b, i).start()

    def pieces(b):
        made = []
        for k in range(m):
            strip = g * m + k
            src = d_buf.at[b, pl.ds(k * sr * CD, sr * CD)]
            dst = r_buf.at[b, s]
            remote = functools.partial(
                pltpu.make_async_remote_copy,
                src_ref=src,
                dst_ref=dst,
                send_sem=rsend.at[b, k],
                recv_sem=rmain.at[b, s],
                device_id=(0, strip),
                device_id_type=MESH,
            )
            local = functools.partial(pltpu.make_async_copy, src, dst, rmain.at[b, s])
            own = (g == 0) & (s == strip)
            made.append((~own, own, remote, local))
        return made

    def conv_rows(buf, first_col, size, weight, sel):
        data = [
            buf[sel(first_col + j, size)].reshape(size * pitch, K1) for j in range(3)
        ]
        data = jnp.concatenate(data, axis=1)
        part = [
            jnp.dot(
                data,
                weight[:, a * K1 : (a + 1) * K1],
                preferred_element_type=jnp.float32,
            )
            for a in range(3)
        ]
        part = [p.reshape(size, pitch, K1) for p in part]
        return pltpu.roll(part[0], 1, 1) + part[1] + pltpu.roll(part[2], pitch - 1, 1)

    size1 = fits(C + 2, pitch, 320)
    size2 = fits(C, pitch, 400)

    def stem(b):
        for i, (dg, ds) in enumerate(DIRS):

            @pl.when(inside(g - dg, s - ds))
            def _():
                border(b, i).wait_recv()

        low = lax.broadcasted_iota(jnp.int32, (C + 4, EDGE, K1), 1) < EDGE // 2
        x_buf[b, :, R:] = jnp.where(
            low, bot_buf[b].astype(jnp.float32), top_buf[b].astype(jnp.float32)
        ).astype(jnp.bfloat16)
        if b == 0:
            weights_wait(0)

        def one(t, carry):
            c0 = t * size1
            conv = conv_rows(
                x_buf, c0, size1, wf_v, lambda at, size: (b, pl.ds(at, size))
            )
            inner = x_buf[b, pl.ds(c0 + 1, size1)].astype(jnp.float32)
            value = jnp.maximum(inner + conv, 0.0)
            col = lax.broadcasted_iota(jnp.int32, (size1, pitch, K1), 0) + (
                s * C + c0 - 1
            )
            row = lax.broadcasted_iota(jnp.int32, (size1, pitch, K1), 1)
            row = jnp.where(row < R + EDGE // 2, row, row - pitch) + g * R
            keep = (col >= 0) & (col < N * C) & (row >= 0) & (row < S * R)
            f_buf[pl.ds(c0, size1)] = jnp.where(keep, value, 0.0).astype(jnp.bfloat16)
            return carry

        lax.fori_loop(0, (C + 2) // size1, one, 0)
        if b == 0:
            weights_wait(1)

        def two(t, carry):
            c0 = t * size2
            conv = conv_rows(f_buf, c0, size2, ws_v, lambda at, size: (pl.ds(at, size),))
            conv = conv[:, :R]
            inner = f_buf[pl.ds(c0 + 1, size2), :R].astype(jnp.float32)
            value = jnp.maximum(inner + conv, 0.0)
            at = pl.multiple_of(c0 * R, R)
            value = value.reshape(size2 * R, K1)
            for q in range(K1 // 128):
                s_buf[q, pl.ds(at, size2 * R), :] = value[:, q * 128 : (q + 1) * 128]
            return carry

        lax.fori_loop(0, C // size2, two, 0)
        if b == 0:
            weights_wait(2)
        taps = []
        for a in range(2):
            picked = jnp.concatenate(
                [
                    s_buf[q, pl.ds(a, C * RD, stride=2), :]
                    for q in range(K1 // 128)
                ],
                axis=1,
            )
            picked = picked.reshape(CD, 2, RD, K1)
            for c in range(2):
                taps.append(picked[:, c].reshape(CD * RD, K1).astype(jnp.bfloat16))
        reduced = jnp.dot(
            jnp.concatenate(taps, axis=1), wd_v[...], preferred_element_type=jnp.float32
        )
        reduced = jnp.maximum(reduced, 0.0).astype(jnp.bfloat16)
        d_buf[b] = jnp.dot(
            swap(CD, RD), reduced, preferred_element_type=jnp.float32
        ).astype(jnp.bfloat16)
        for away, home, remote, local in pieces(b):

            @pl.when(away)
            def _():
                remote().start()

            @pl.when(home)
            def _():
                local().start()

    for b in range(B):
        stem(b)
    weights_wait(3)

    def strip_copy(b, low):
        src, dst, to = (1, sr + 1, s - 1) if low else (sr, 0, s + 1)
        i = 0 if low else 1
        return pltpu.make_async_remote_copy(
            src_ref=z_buf.at[b, pl.ds(src, 1)],
            dst_ref=z_buf.at[b, pl.ds(dst, 1)],
            send_sem=zsend.at[b, i],
            recv_sem=erecv.at[b, i],
            device_id=(g, to),
            device_id_type=MESH,
        )

    def arrive(b):
        def waits(src, carry):
            part = r_buf.at[b, src]
            pltpu.make_async_copy(part, part, rmain.at[b, src]).wait()
            return carry

        lax.fori_loop(0, N, waits, 0)
        group = max(1, EDGE // CD)
        for q in range(N // group):
            parts = [
                r_buf[b, q * group + j].astype(jnp.float32).reshape(sr, CD, K2)
                for j in range(group)
            ]
            whole = parts[0] if group == 1 else jnp.concatenate(parts, axis=1)
            z_buf[b, 1 : sr + 1, q * group * CD : (q + 1) * group * CD] = whole.astype(
                jnp.bfloat16
            )

        @pl.when(s > 0)
        def _():
            strip_copy(b, True).start()

        @pl.when(s < N - 1)
        def _():
            strip_copy(b, False).start()

    def chunk_copy(b, k):
        rows = pl.ds(k * cr, cr)
        return pltpu.make_async_remote_copy(
            src_ref=o_buf.at[b, rows],
            dst_ref=z_buf.at[b, pl.ds(k * cr + 1, cr)],
            send_sem=csend.at[b, k],
            recv_sem=crecv.at[b, k],
            device_id=(g + 1, s),
            device_id_type=MESH,
        )

    def edge_copy(b, low):
        src, dst, to = (0, sr + 1, s - 1) if low else (sr - 1, 0, s + 1)
        i = 0 if low else 1
        return pltpu.make_async_remote_copy(
            src_ref=o_buf.at[b, pl.ds(src, 1)],
            dst_ref=z_buf.at[b, pl.ds(dst, 1)],
            send_sem=esend.at[b, i],
            recv_sem=erecv.at[b, i],
            device_id=(g + 1, to),
            device_id_type=MESH,
        )

    def out_copy(b, k):
        rows = pl.ds(k * cr, cr)
        return pltpu.make_async_copy(
            o_buf.at[b, rows], out.at[0, b, rows], osem.at[b, k]
        )

    span = cr * cols
    width = 256

    def section(b, p):
        k = jnp.where(p == n - 1, n - 1, jnp.where(p == n - 2, 0, p + 1))

        @pl.when(g > 0)
        def _():
            @pl.when(p == 0)
            def _():
                for j in range(3):
                    chunk_copy(b, j).wait_recv()

            @pl.when((p > 0) & (p < n - 2))
            def _():
                chunk_copy(b, p + 2).wait_recv()

        @pl.when((p == n - 2) & (s > 0))
        def _():
            edge_copy(b, False).wait_recv()

        @pl.when((p == n - 1) & (s < N - 1))
        def _():
            edge_copy(b, True).wait_recv()

        data = jnp.concatenate(
            [z_buf[b, pl.ds(k * cr + a, cr)].reshape(span, K2) for a in range(3)],
            axis=1,
        )
        place = lax.broadcasted_iota(jnp.int32, (cr, cols, width), 1).reshape(span, width)
        for q in range(K2 // width):
            part = [
                jnp.dot(
                    data,
                    wsec_v[:, c * K2 + q * width : c * K2 + (q + 1) * width],
                    preferred_element_type=jnp.float32,
                )
                for c in range(3)
            ]
            left = jnp.where(place == 0, 0.0, pltpu.roll(part[0], 1, 0))
            right = jnp.where(place == cols - 1, 0.0, pltpu.roll(part[2], span - 1, 0))
            inner = z_buf[
                b, pl.ds(k * cr + 1, cr), :, q * width : (q + 1) * width
            ].reshape(span, width)
            value = jnp.maximum(inner.astype(jnp.float32) + left + part[1] + right, 0.0)
            o_buf[b, pl.ds(k * cr, cr), :, q * width : (q + 1) * width] = value.astype(
                jnp.bfloat16
            ).reshape(cr, cols, width)
        out_copy(b, k).start()

        @pl.when(g < S - 1)
        def _():
            @pl.when((k == 0) & (s > 0))
            def _():
                edge_copy(b, True).start()

            @pl.when((k == n - 1) & (s < N - 1))
            def _():
                edge_copy(b, False).start()

            chunk_copy(b, k).start()

    for b in range(B):

        @pl.when(g == 0)
        def _():
            arrive(b)

        def step(p, carry):
            section(b, p)
            return carry

        lax.fori_loop(0, n, step, 0)

    for b in range(B):
        for i, (dg, ds) in enumerate(DIRS):

            @pl.when(inside(g + dg, s + ds))
            def _():
                border(b, i).wait_send()

        for away, home, remote, local in pieces(b):

            @pl.when(away)
            def _():
                remote().wait_send()

        @pl.when((g == 0) & (s > 0))
        def _():
            strip_copy(b, True).wait_send()

        @pl.when((g == 0) & (s < N - 1))
        def _():
            strip_copy(b, False).wait_send()

        @pl.when(g < S - 1)
        def _():
            @pl.when(s > 0)
            def _():
                edge_copy(b, True).wait_send()

            @pl.when(s < N - 1)
            def _():
                edge_copy(b, False).wait_send()

            for k in range(n):
                chunk_copy(b, k).wait_send()

        for k in range(n):
            out_copy(b, k).wait()


def shards(S, N, features, weight_first, weight_second, weight_down, section_weights):
    B, R, C, K1 = features.shape
    K2 = weight_down.shape[3]
    RD, CD = R // 2, C // 2
    m = N // S
    sr = RD // m
    cols = CD * N
    n = sr // max(1, 256 // cols)
    pitch = R + EDGE
    bf16, f32 = jnp.bfloat16, jnp.float32
    dma = pltpu.SemaphoreType.DMA
    anywhere = pl.BlockSpec(memory_space=pl.ANY)
    flops = 2 * B * (R * C * 18 * K1 * K1 + RD * CD * 4 * K1 * K2 + sr * cols * 9 * K2 * K2)
    return pl.pallas_call(
        functools.partial(kernel, (S, N, B, R, C, K1, K2)),
        out_shape=jax.ShapeDtypeStruct((1, B, sr, cols, K2), bf16),
        in_specs=[pl.BlockSpec(memory_space=pltpu.HBM)] * 5,
        out_specs=anywhere,
        scratch_shapes=[
            pltpu.VMEM((B, R, C, K1), bf16),
            pltpu.VMEM((B, C + 4, EDGE, K1), bf16),
            pltpu.VMEM((B, C + 4, EDGE, K1), bf16),
            pltpu.VMEM((B, C + 4, pitch, K1), bf16),
            pltpu.VMEM((C + 2, pitch, K1), bf16),
            pltpu.VMEM((K1 // 128, C * R, 128), f32),
            pltpu.VMEM((B, RD * CD, K2), bf16),
            pltpu.VMEM((B, N, sr * CD, K2), bf16),
            pltpu.VMEM((B, sr + 2, cols, K2), bf16),
            pltpu.VMEM((B, sr, cols, K2), bf16),
            pltpu.VMEM((3 * K1, 3 * K1), bf16),
            pltpu.VMEM((3 * K1, 3 * K1), bf16),
            pltpu.VMEM((4 * K1, K2), bf16),
            pltpu.VMEM((3 * K2, 3 * K2), bf16),
            dma((31,)),
            dma((B,)),
            dma((B, 8)),
            dma((B, 8)),
            dma((B, m)),
            dma((B, N)),
            dma((B, n)),
            dma((B, n)),
            dma((B, 2)),
            dma((B, 2)),
            dma((B, 2)),
            dma((B, n)),
        ],
        compiler_params=pltpu.CompilerParams(
            collective_id=0, has_side_effects=True, vmem_limit_bytes=56 * 1024 * 1024
        ),
        cost_estimate=pl.CostEstimate(
            flops=flops, bytes_accessed=16 * 1024 * 1024, transcendentals=0
        ),
    )(
        features,
        weight_first,
        weight_second,
        weight_down,
        section_weights,
    )


def solution(mesh):
    return jax.shard_map(
        functools.partial(shards, mesh.shape["segment"], mesh.shape["strip"]),
        mesh=mesh,
        in_specs=(
            P(None, "segment", "strip", None),
            P(),
            P(),
            P(),
            P("segment", None, None, None, None),
        ),
        out_specs=P("segment", None, "strip", None, None),
        check_vma=False,
    )
```

```python
import functools

import jax
import jax.numpy as jnp
from jax import lax
from jax.experimental import pallas as pl
from jax.experimental.pallas import tpu as pltpu
from jax.sharding import PartitionSpec as P

MESH = pl.DeviceIdType.MESH
EDGE = 16
DIRS = [(dg, ds) for dg in (-1, 0, 1) for ds in (-1, 0, 1) if (dg, ds) != (0, 0)]


def fits(count, pitch, limit):
    best = 1
    for size in range(1, count + 1):
        if count % size == 0 and size * pitch <= limit:
            best = size
    return best


def kernel(
    dims,
    feat,
    wf,
    ws,
    wd,
    wsec,
    out,
    raw_buf,
    top_buf,
    bot_buf,
    x_buf,
    f_buf,
    s_buf,
    d_buf,
    r_buf,
    z_buf,
    o_buf,
    wf_v,
    ws_v,
    wd_v,
    wsec_v,
    wsem,
    fsem,
    hsend,
    hrecv,
    rsend,
    rmain,
    csend,
    crecv,
    zsend,
    esend,
    erecv,
    osem,
):
    S, N, B, R, C, K1, K2 = dims
    RD, CD = R // 2, C // 2
    m = N // S
    sr = RD // m
    cols = CD * N
    cr = max(1, 128 // cols)
    n = sr // cr
    pitch = R + EDGE
    g = lax.axis_index("segment")
    s = lax.axis_index("strip")

    copies = []
    for a in range(3):
        for c in range(3):
            copies.append(
                (0, wf.at[a, c], wf_v.at[pl.ds(c * K1, K1), pl.ds(a * K1, K1)])
            )
    for a in range(3):
        for c in range(3):
            copies.append(
                (1, ws.at[a, c], ws_v.at[pl.ds(c * K1, K1), pl.ds(a * K1, K1)])
            )
    for a in range(2):
        for c in range(2):
            copies.append((2, wd.at[a, c], wd_v.at[pl.ds((2 * a + c) * K1, K1)]))
    for a in range(3):
        for c in range(3):
            copies.append(
                (3, wsec.at[0, a, c], wsec_v.at[pl.ds(a * K2, K2), pl.ds(c * K2, K2)])
            )
    weights = [
        (group, pltpu.make_async_copy(src, dst, wsem.at[i]))
        for i, (group, src, dst) in enumerate(copies)
    ]

    def weights_wait(which):
        for group, copy in weights:
            if group == which:
                copy.wait()

    centre = [
        pltpu.make_async_copy(
            feat.at[b], raw_buf.at[b], fsem.at[b]
        )
        for b in range(B)
    ]
    for copy in centre:
        copy.start()
    for _, copy in weights:
        copy.start()

    zero = jnp.bfloat16(0)
    x_buf[:, 0:2] = jnp.full((B, 2, pitch, K1), zero)
    x_buf[:, C + 2 : C + 4] = jnp.full((B, 2, pitch, K1), zero)
    top_buf[...] = jnp.full((B, C + 4, EDGE, K1), zero)
    bot_buf[...] = jnp.full((B, C + 4, EDGE, K1), zero)
    z_buf[:, 0] = jnp.full((B, cols, K2), zero)
    z_buf[:, sr + 1] = jnp.full((B, cols, K2), zero)

    def swap(outer, inner):
        shape = (inner, outer, outer * inner)
        i, j, q = [lax.broadcasted_iota(jnp.int32, shape, d) for d in range(3)]
        hot = jnp.where(q == j * inner + i, 1.0, 0.0)
        return hot.reshape(outer * inner, outer * inner).astype(jnp.bfloat16)

    turn = swap(EDGE, C)
    for b in range(B):
        centre[b].wait()
        for q in range(R // EDGE):
            block = raw_buf[b, q * EDGE : (q + 1) * EDGE].reshape(EDGE * C, K1)
            block = jnp.dot(turn, block, preferred_element_type=jnp.float32)
            x_buf[b, 2 : C + 2, q * EDGE : (q + 1) * EDGE] = block.astype(
                jnp.bfloat16
            ).reshape(C, EDGE, K1)

    barrier = pltpu.get_barrier_semaphore()
    total = S * N
    me = g * N + s

    def greet(k, carry):
        other = lax.rem(me + k, total)
        pl.semaphore_signal(
            barrier,
            inc=1,
            device_id=(lax.div(other, N), lax.rem(other, N)),
            device_id_type=MESH,
        )
        return carry

    lax.fori_loop(1, total, greet, 0)
    pl.semaphore_wait(barrier, total - 1)

    def inside(gg, ss):
        return (gg >= 0) & (gg < S) & (ss >= 0) & (ss < N)

    row_src = {-1: (0, EDGE), 0: (0, R), 1: (R - EDGE, EDGE)}
    col_src = {-1: (2, 2), 0: (2, C), 1: (C, 2)}
    col_dst = {-1: C + 2, 0: 2, 1: 0}

    def border(b, i):
        dg, ds = DIRS[i]
        r0, rn = row_src[dg]
        c0, cn = col_src[ds]
        where = pl.ds(col_dst[ds], cn)
        if dg == 0:
            dst = x_buf.at[b, where, pl.ds(0, R)]
        else:
            dst = (top_buf if dg == 1 else bot_buf).at[b, where]
        return pltpu.make_async_remote_copy(
            src_ref=x_buf.at[b, pl.ds(c0, cn), pl.ds(r0, rn)],
            dst_ref=dst,
            send_sem=hsend.at[b, i],
            recv_sem=hrecv.at[b, i],
            device_id=(g + dg, s + ds),
            device_id_type=MESH,
        )

    for b in range(B):
        for i, (dg, ds) in enumerate(DIRS):

            @pl.when(inside(g + dg, s + ds))
            def _():
                border(b, i).start()

    def pieces(b):
        made = []
        for k in range(m):
            strip = g * m + k
            src = d_buf.at[b, pl.ds(k * sr * CD, sr * CD)]
            dst = r_buf.at[b, s]
            remote = functools.partial(
                pltpu.make_async_remote_copy,
                src_ref=src,
                dst_ref=dst,
                send_sem=rsend.at[b, k],
                recv_sem=rmain.at[b, s],
                device_id=(0, strip),
                device_id_type=MESH,
            )
            local = functools.partial(pltpu.make_async_copy, src, dst, rmain.at[b, s])
            own = (g == 0) & (s == strip)
            made.append((~own, own, remote, local))
        return made

    def conv_rows(buf, first_col, size, weight, sel):
        data = [
            buf[sel(first_col + j, size)].reshape(size * pitch, K1) for j in range(3)
        ]
        data = jnp.concatenate(data, axis=1)
        part = [
            jnp.dot(
                data,
                weight[:, a * K1 : (a + 1) * K1],
                preferred_element_type=jnp.float32,
            )
            for a in range(3)
        ]
        part = [p.reshape(size, pitch, K1) for p in part]
        return pltpu.roll(part[0], 1, 1) + part[1] + pltpu.roll(part[2], pitch - 1, 1)

    size1 = fits(C + 2, pitch, 320)
    size2 = fits(C, pitch, 400)

    def stem(b):
        for i, (dg, ds) in enumerate(DIRS):

            @pl.when(inside(g - dg, s - ds))
            def _():
                border(b, i).wait_recv()

        low = lax.broadcasted_iota(jnp.int32, (C + 4, EDGE, K1), 1) < EDGE // 2
        x_buf[b, :, R:] = jnp.where(
            low, bot_buf[b].astype(jnp.float32), top_buf[b].astype(jnp.float32)
        ).astype(jnp.bfloat16)
        if b == 0:
            weights_wait(0)

        def one(t, carry):
            c0 = t * size1
            conv = conv_rows(
                x_buf, c0, size1, wf_v, lambda at, size: (b, pl.ds(at, size))
            )
            inner = x_buf[b, pl.ds(c0 + 1, size1)].astype(jnp.float32)
            value = jnp.maximum(inner + conv, 0.0)
            col = lax.broadcasted_iota(jnp.int32, (size1, pitch, K1), 0) + (
                s * C + c0 - 1
            )
            row = lax.broadcasted_iota(jnp.int32, (size1, pitch, K1), 1)
            row = jnp.where(row < R + EDGE // 2, row, row - pitch) + g * R
            keep = (col >= 0) & (col < N * C) & (row >= 0) & (row < S * R)
            f_buf[pl.ds(c0, size1)] = jnp.where(keep, value, 0.0).astype(jnp.bfloat16)
            return carry

        lax.fori_loop(0, (C + 2) // size1, one, 0)
        if b == 0:
            weights_wait(1)

        def two(t, carry):
            c0 = t * size2
            conv = conv_rows(f_buf, c0, size2, ws_v, lambda at, size: (pl.ds(at, size),))
            conv = conv[:, :R]
            inner = f_buf[pl.ds(c0 + 1, size2), :R].astype(jnp.float32)
            value = jnp.maximum(inner + conv, 0.0)
            at = pl.multiple_of(c0 * R, R)
            value = value.reshape(size2 * R, K1)
            for q in range(K1 // 128):
                s_buf[q, pl.ds(at, size2 * R), :] = value[:, q * 128 : (q + 1) * 128]
            return carry

        lax.fori_loop(0, C // size2, two, 0)
        if b == 0:
            weights_wait(2)
        taps = []
        for a in range(2):
            picked = jnp.concatenate(
                [
                    s_buf[q, pl.ds(a, C * RD, stride=2), :]
                    for q in range(K1 // 128)
                ],
                axis=1,
            )
            picked = picked.reshape(CD, 2, RD, K1)
            for c in range(2):
                taps.append(picked[:, c].reshape(CD * RD, K1).astype(jnp.bfloat16))
        reduced = jnp.dot(
            jnp.concatenate(taps, axis=1), wd_v[...], preferred_element_type=jnp.float32
        )
        reduced = jnp.maximum(reduced, 0.0).astype(jnp.bfloat16)
        d_buf[b] = jnp.dot(
            swap(CD, RD), reduced, preferred_element_type=jnp.float32
        ).astype(jnp.bfloat16)
        for away, home, remote, local in pieces(b):

            @pl.when(away)
            def _():
                remote().start()

            @pl.when(home)
            def _():
                local().start()

    for b in range(B):
        stem(b)
    weights_wait(3)

    def strip_copy(b, low):
        src, dst, to = (1, sr + 1, s - 1) if low else (sr, 0, s + 1)
        i = 0 if low else 1
        return pltpu.make_async_remote_copy(
            src_ref=z_buf.at[b, pl.ds(src, 1)],
            dst_ref=z_buf.at[b, pl.ds(dst, 1)],
            send_sem=zsend.at[b, i],
            recv_sem=erecv.at[b, i],
            device_id=(g, to),
            device_id_type=MESH,
        )

    def arrive(b):
        def waits(src, carry):
            part = r_buf.at[b, src]
            pltpu.make_async_copy(part, part, rmain.at[b, src]).wait()
            return carry

        lax.fori_loop(0, N, waits, 0)
        group = max(1, EDGE // CD)
        for q in range(N // group):
            parts = [
                r_buf[b, q * group + j].astype(jnp.float32).reshape(sr, CD, K2)
                for j in range(group)
            ]
            whole = parts[0] if group == 1 else jnp.concatenate(parts, axis=1)
            z_buf[b, 1 : sr + 1, q * group * CD : (q + 1) * group * CD] = whole.astype(
                jnp.bfloat16
            )

        @pl.when(s > 0)
        def _():
            strip_copy(b, True).start()

        @pl.when(s < N - 1)
        def _():
            strip_copy(b, False).start()

    def chunk_copy(b, k):
        rows = pl.ds(k * cr, cr)
        return pltpu.make_async_remote_copy(
            src_ref=o_buf.at[b, rows],
            dst_ref=z_buf.at[b, pl.ds(k * cr + 1, cr)],
            send_sem=csend.at[b, k],
            recv_sem=crecv.at[b, k],
            device_id=(g + 1, s),
            device_id_type=MESH,
        )

    def edge_copy(b, low):
        src, dst, to = (0, sr + 1, s - 1) if low else (sr - 1, 0, s + 1)
        i = 0 if low else 1
        return pltpu.make_async_remote_copy(
            src_ref=o_buf.at[b, pl.ds(src, 1)],
            dst_ref=z_buf.at[b, pl.ds(dst, 1)],
            send_sem=esend.at[b, i],
            recv_sem=erecv.at[b, i],
            device_id=(g + 1, to),
            device_id_type=MESH,
        )

    def out_copy(b, k):
        rows = pl.ds(k * cr, cr)
        return pltpu.make_async_copy(
            o_buf.at[b, rows], out.at[0, b, rows], osem.at[b, k]
        )

    span = cr * cols
    width = 256

    def section(b, p):
        k = jnp.where(p == n - 1, n - 1, jnp.where(p == n - 2, 0, p + 1))

        @pl.when(g > 0)
        def _():
            @pl.when(p == 0)
            def _():
                for j in range(3):
                    chunk_copy(b, j).wait_recv()

            @pl.when((p > 0) & (p < n - 2))
            def _():
                chunk_copy(b, p + 2).wait_recv()

        @pl.when((p == n - 2) & (s > 0))
        def _():
            edge_copy(b, False).wait_recv()

        @pl.when((p == n - 1) & (s < N - 1))
        def _():
            edge_copy(b, True).wait_recv()

        data = jnp.concatenate(
            [z_buf[b, pl.ds(k * cr + a, cr)].reshape(span, K2) for a in range(3)],
            axis=1,
        )
        place = lax.broadcasted_iota(jnp.int32, (cr, cols, width), 1).reshape(span, width)
        for q in range(K2 // width):
            part = [
                jnp.dot(
                    data,
                    wsec_v[:, c * K2 + q * width : c * K2 + (q + 1) * width],
                    preferred_element_type=jnp.float32,
                )
                for c in range(3)
            ]
            left = jnp.where(place == 0, 0.0, pltpu.roll(part[0], 1, 0))
            right = jnp.where(place == cols - 1, 0.0, pltpu.roll(part[2], span - 1, 0))
            inner = z_buf[
                b, pl.ds(k * cr + 1, cr), :, q * width : (q + 1) * width
            ].reshape(span, width)
            value = jnp.maximum(inner.astype(jnp.float32) + left + part[1] + right, 0.0)
            o_buf[b, pl.ds(k * cr, cr), :, q * width : (q + 1) * width] = value.astype(
                jnp.bfloat16
            ).reshape(cr, cols, width)
        out_copy(b, k).start()

        @pl.when(g < S - 1)
        def _():
            @pl.when((k == 0) & (s > 0))
            def _():
                edge_copy(b, True).start()

            @pl.when((k == n - 1) & (s < N - 1))
            def _():
                edge_copy(b, False).start()

            chunk_copy(b, k).start()

    for b in range(B):

        @pl.when(g == 0)
        def _():
            arrive(b)

        def step(p, carry):
            section(b, p)
            return carry

        lax.fori_loop(0, n, step, 0)

    for b in range(B):
        for i, (dg, ds) in enumerate(DIRS):

            @pl.when(inside(g + dg, s + ds))
            def _():
                border(b, i).wait_send()

        for away, home, remote, local in pieces(b):

            @pl.when(away)
            def _():
                remote().wait_send()

        @pl.when((g == 0) & (s > 0))
        def _():
            strip_copy(b, True).wait_send()

        @pl.when((g == 0) & (s < N - 1))
        def _():
            strip_copy(b, False).wait_send()

        @pl.when(g < S - 1)
        def _():
            @pl.when(s > 0)
            def _():
                edge_copy(b, True).wait_send()

            @pl.when(s < N - 1)
            def _():
                edge_copy(b, False).wait_send()

            for k in range(n):
                chunk_copy(b, k).wait_send()

        for k in range(n):
            out_copy(b, k).wait()


def shards(S, N, features, weight_first, weight_second, weight_down, section_weights):
    B, R, C, K1 = features.shape
    K2 = weight_down.shape[3]
    RD, CD = R // 2, C // 2
    m = N // S
    sr = RD // m
    cols = CD * N
    n = sr // max(1, 128 // cols)
    pitch = R + EDGE
    bf16, f32 = jnp.bfloat16, jnp.float32
    dma = pltpu.SemaphoreType.DMA
    anywhere = pl.BlockSpec(memory_space=pl.ANY)
    flops = 2 * B * (R * C * 18 * K1 * K1 + RD * CD * 4 * K1 * K2 + sr * cols * 9 * K2 * K2)
    return pl.pallas_call(
        functools.partial(kernel, (S, N, B, R, C, K1, K2)),
        out_shape=jax.ShapeDtypeStruct((1, B, sr, cols, K2), bf16),
        in_specs=[pl.BlockSpec(memory_space=pltpu.HBM)] * 5,
        out_specs=anywhere,
        scratch_shapes=[
            pltpu.VMEM((B, R, C, K1), bf16),
            pltpu.VMEM((B, C + 4, EDGE, K1), bf16),
            pltpu.VMEM((B, C + 4, EDGE, K1), bf16),
            pltpu.VMEM((B, C + 4, pitch, K1), bf16),
            pltpu.VMEM((C + 2, pitch, K1), bf16),
            pltpu.VMEM((K1 // 128, C * R, 128), f32),
            pltpu.VMEM((B, RD * CD, K2), bf16),
            pltpu.VMEM((B, N, sr * CD, K2), bf16),
            pltpu.VMEM((B, sr + 2, cols, K2), bf16),
            pltpu.VMEM((B, sr, cols, K2), bf16),
            pltpu.VMEM((3 * K1, 3 * K1), bf16),
            pltpu.VMEM((3 * K1, 3 * K1), bf16),
            pltpu.VMEM((4 * K1, K2), bf16),
            pltpu.VMEM((3 * K2, 3 * K2), bf16),
            dma((31,)),
            dma((B,)),
            dma((B, 8)),
            dma((B, 8)),
            dma((B, m)),
            dma((B, N)),
            dma((B, n)),
            dma((B, n)),
            dma((B, 2)),
            dma((B, 2)),
            dma((B, 2)),
            dma((B, n)),
        ],
        compiler_params=pltpu.CompilerParams(
            collective_id=0, has_side_effects=True, vmem_limit_bytes=56 * 1024 * 1024
        ),
        cost_estimate=pl.CostEstimate(
            flops=flops, bytes_accessed=16 * 1024 * 1024, transcendentals=0
        ),
    )(
        features,
        weight_first,
        weight_second,
        weight_down,
        section_weights,
    )


def solution(mesh):
    return jax.shard_map(
        functools.partial(shards, mesh.shape["segment"], mesh.shape["strip"]),
        mesh=mesh,
        in_specs=(
            P(None, "segment", "strip", None),
            P(),
            P(),
            P(),
            P("segment", None, None, None, None),
        ),
        out_specs=P("segment", None, "strip", None, None),
        check_vma=False,
    )
```

```python
import functools

import jax
import jax.numpy as jnp
from jax import lax
from jax.experimental import pallas as pl
from jax.experimental.pallas import tpu as pltpu
from jax.sharding import PartitionSpec as P

MESH = pl.DeviceIdType.MESH
EDGE = 16
DIRS = [(dg, ds) for dg in (-1, 0, 1) for ds in (-1, 0, 1) if (dg, ds) != (0, 0)]


def fits(count, pitch, limit):
    best = 1
    for size in range(1, count + 1):
        if count % size == 0 and size * pitch <= limit:
            best = size
    return best


def kernel(
    dims,
    feat,
    wf,
    ws,
    wd,
    wsec,
    out,
    raw_buf,
    top_buf,
    bot_buf,
    x_buf,
    f_buf,
    s_buf,
    d_buf,
    r_buf,
    z_buf,
    o_buf,
    wf_v,
    ws_v,
    wd_v,
    wsec_v,
    wsem,
    fsem,
    hsend,
    hrecv,
    rsend,
    rmain,
    csend,
    crecv,
    zsend,
    esend,
    erecv,
    osem,
):
    S, N, B, R, C, K1, K2 = dims
    RD, CD = R // 2, C // 2
    m = N // S
    sr = RD // m
    cols = CD * N
    cr = max(1, 256 // cols)
    n = sr // cr
    pitch = R + EDGE
    g = lax.axis_index("segment")
    s = lax.axis_index("strip")

    copies = []
    for a in range(3):
        for c in range(3):
            copies.append(
                (0, wf.at[a, c], wf_v.at[pl.ds(c * K1, K1), pl.ds(a * K1, K1)])
            )
    for a in range(3):
        for c in range(3):
            copies.append(
                (1, ws.at[a, c], ws_v.at[pl.ds(c * K1, K1), pl.ds(a * K1, K1)])
            )
    for a in range(2):
        for c in range(2):
            copies.append((2, wd.at[a, c], wd_v.at[pl.ds((2 * a + c) * K1, K1)]))
    for a in range(3):
        for c in range(3):
            copies.append(
                (3, wsec.at[0, a, c], wsec_v.at[pl.ds(a * K2, K2), pl.ds(c * K2, K2)])
            )
    weights = [
        (group, pltpu.make_async_copy(src, dst, wsem.at[i]))
        for i, (group, src, dst) in enumerate(copies)
    ]

    def weights_wait(which):
        for group, copy in weights:
            if group == which:
                copy.wait()

    centre = [
        pltpu.make_async_copy(
            feat.at[b], raw_buf.at[b], fsem.at[b]
        )
        for b in range(B)
    ]
    for copy in centre:
        copy.start()
    for _, copy in weights:
        copy.start()

    zero = jnp.bfloat16(0)
    x_buf[:, 0:2] = jnp.full((B, 2, pitch, K1), zero)
    x_buf[:, C + 2 : C + 4] = jnp.full((B, 2, pitch, K1), zero)
    top_buf[...] = jnp.full((B, C + 4, EDGE, K1), zero)
    bot_buf[...] = jnp.full((B, C + 4, EDGE, K1), zero)
    z_buf[:, 0] = jnp.full((B, cols, K2), zero)
    z_buf[:, sr + 1] = jnp.full((B, cols, K2), zero)

    def swap(outer, inner):
        shape = (inner, outer, outer * inner)
        i, j, q = [lax.broadcasted_iota(jnp.int32, shape, d) for d in range(3)]
        hot = jnp.where(q == j * inner + i, 1.0, 0.0)
        return hot.reshape(outer * inner, outer * inner).astype(jnp.bfloat16)

    turn = swap(EDGE, C)
    for b in range(B):
        centre[b].wait()
        for q in range(R // EDGE):
            block = raw_buf[b, q * EDGE : (q + 1) * EDGE].reshape(EDGE * C, K1)
            block = jnp.dot(turn, block, preferred_element_type=jnp.float32)
            x_buf[b, 2 : C + 2, q * EDGE : (q + 1) * EDGE] = block.astype(
                jnp.bfloat16
            ).reshape(C, EDGE, K1)

    barrier = pltpu.get_barrier_semaphore()
    total = S * N
    me = g * N + s

    def greet(k, carry):
        other = lax.rem(me + k, total)
        pl.semaphore_signal(
            barrier,
            inc=1,
            device_id=(lax.div(other, N), lax.rem(other, N)),
            device_id_type=MESH,
        )
        return carry

    lax.fori_loop(1, total, greet, 0)
    pl.semaphore_wait(barrier, total - 1)

    def inside(gg, ss):
        return (gg >= 0) & (gg < S) & (ss >= 0) & (ss < N)

    row_src = {-1: (0, EDGE), 0: (0, R), 1: (R - EDGE, EDGE)}
    col_src = {-1: (2, 2), 0: (2, C), 1: (C, 2)}
    col_dst = {-1: C + 2, 0: 2, 1: 0}

    def border(b, i):
        dg, ds = DIRS[i]
        r0, rn = row_src[dg]
        c0, cn = col_src[ds]
        where = pl.ds(col_dst[ds], cn)
        if dg == 0:
            dst = x_buf.at[b, where, pl.ds(0, R)]
        else:
            dst = (top_buf if dg == 1 else bot_buf).at[b, where]
        return pltpu.make_async_remote_copy(
            src_ref=x_buf.at[b, pl.ds(c0, cn), pl.ds(r0, rn)],
            dst_ref=dst,
            send_sem=hsend.at[b, i],
            recv_sem=hrecv.at[b, i],
            device_id=(g + dg, s + ds),
            device_id_type=MESH,
        )

    for b in range(B):
        for i, (dg, ds) in enumerate(DIRS):

            @pl.when(inside(g + dg, s + ds))
            def _():
                border(b, i).start()

    def pieces(b):
        made = []
        for k in range(m):
            strip = g * m + k
            src = d_buf.at[b, pl.ds(k * sr * CD, sr * CD)]
            dst = r_buf.at[b, s]
            remote = functools.partial(
                pltpu.make_async_remote_copy,
                src_ref=src,
                dst_ref=dst,
                send_sem=rsend.at[b, k],
                recv_sem=rmain.at[b, s],
                device_id=(0, strip),
                device_id_type=MESH,
            )
            local = functools.partial(pltpu.make_async_copy, src, dst, rmain.at[b, s])
            own = (g == 0) & (s == strip)
            made.append((~own, own, remote, local))
        return made

    def conv_rows(buf, first_col, size, weight, sel):
        data = [
            buf[sel(first_col + j, size)].reshape(size * pitch, K1) for j in range(3)
        ]
        data = jnp.concatenate(data, axis=1)
        part = [
            jnp.dot(
                data,
                weight[:, a * K1 : (a + 1) * K1],
                preferred_element_type=jnp.float32,
            )
            for a in range(3)
        ]
        part = [p.reshape(size, pitch, K1) for p in part]
        return pltpu.roll(part[0], 1, 1) + part[1] + pltpu.roll(part[2], pitch - 1, 1)

    size1 = fits(C + 2, pitch, 320)
    size2 = fits(C, pitch, 400)

    def stem(b):
        for i, (dg, ds) in enumerate(DIRS):

            @pl.when(inside(g - dg, s - ds))
            def _():
                border(b, i).wait_recv()

        low = lax.broadcasted_iota(jnp.int32, (C + 4, EDGE, K1), 1) < EDGE // 2
        x_buf[b, :, R:] = jnp.where(
            low, bot_buf[b].astype(jnp.float32), top_buf[b].astype(jnp.float32)
        ).astype(jnp.bfloat16)
        if b == 0:
            weights_wait(0)

        def one(t, carry):
            c0 = t * size1
            conv = conv_rows(
                x_buf, c0, size1, wf_v, lambda at, size: (b, pl.ds(at, size))
            )
            inner = x_buf[b, pl.ds(c0 + 1, size1)].astype(jnp.float32)
            value = jnp.maximum(inner + conv, 0.0)
            col = lax.broadcasted_iota(jnp.int32, (size1, pitch, K1), 0) + (
                s * C + c0 - 1
            )
            row = lax.broadcasted_iota(jnp.int32, (size1, pitch, K1), 1)
            row = jnp.where(row < R + EDGE // 2, row, row - pitch) + g * R
            keep = (col >= 0) & (col < N * C) & (row >= 0) & (row < S * R)
            f_buf[pl.ds(c0, size1)] = jnp.where(keep, value, 0.0).astype(jnp.bfloat16)
            return carry

        lax.fori_loop(0, (C + 2) // size1, one, 0)
        if b == 0:
            weights_wait(1)

        def two(t, carry):
            c0 = t * size2
            conv = conv_rows(f_buf, c0, size2, ws_v, lambda at, size: (pl.ds(at, size),))
            conv = conv[:, :R]
            inner = f_buf[pl.ds(c0 + 1, size2), :R].astype(jnp.float32)
            value = jnp.maximum(inner + conv, 0.0)
            at = pl.multiple_of(c0 * R, R)
            value = value.reshape(size2 * R, K1)
            for q in range(K1 // 128):
                s_buf[q, pl.ds(at, size2 * R), :] = value[:, q * 128 : (q + 1) * 128]
            return carry

        lax.fori_loop(0, C // size2, two, 0)
        if b == 0:
            weights_wait(2)
        taps = []
        for a in range(2):
            picked = jnp.concatenate(
                [
                    s_buf[q, pl.ds(a, C * RD, stride=2), :]
                    for q in range(K1 // 128)
                ],
                axis=1,
            )
            picked = picked.reshape(CD, 2, RD, K1)
            for c in range(2):
                taps.append(picked[:, c].reshape(CD * RD, K1).astype(jnp.bfloat16))
        reduced = jnp.dot(
            jnp.concatenate(taps, axis=1), wd_v[...], preferred_element_type=jnp.float32
        )
        reduced = jnp.maximum(reduced, 0.0).astype(jnp.bfloat16)
        d_buf[b] = jnp.dot(
            swap(CD, RD), reduced, preferred_element_type=jnp.float32
        ).astype(jnp.bfloat16)
        if b > 0:
            for away, home, remote, local in pieces(b - 1):

                @pl.when(away)
                def _():
                    remote().wait_send()

        for away, home, remote, local in pieces(b):

            @pl.when(away)
            def _():
                remote().start()

            @pl.when(home)
            def _():
                local().start()

    for b in range(B):
        stem(b)
    weights_wait(3)

    def strip_copy(b, low):
        src, dst, to = (1, sr + 1, s - 1) if low else (sr, 0, s + 1)
        i = 0 if low else 1
        return pltpu.make_async_remote_copy(
            src_ref=z_buf.at[b, pl.ds(src, 1)],
            dst_ref=z_buf.at[b, pl.ds(dst, 1)],
            send_sem=zsend.at[b, i],
            recv_sem=erecv.at[b, i],
            device_id=(g, to),
            device_id_type=MESH,
        )

    def arrive(b):
        def waits(src, carry):
            part = r_buf.at[b, src]
            pltpu.make_async_copy(part, part, rmain.at[b, src]).wait()
            return carry

        lax.fori_loop(0, N, waits, 0)
        group = max(1, EDGE // CD)
        for q in range(N // group):
            parts = [
                r_buf[b, q * group + j].astype(jnp.float32).reshape(sr, CD, K2)
                for j in range(group)
            ]
            whole = parts[0] if group == 1 else jnp.concatenate(parts, axis=1)
            z_buf[b, 1 : sr + 1, q * group * CD : (q + 1) * group * CD] = whole.astype(
                jnp.bfloat16
            )

        @pl.when(s > 0)
        def _():
            strip_copy(b, True).start()

        @pl.when(s < N - 1)
        def _():
            strip_copy(b, False).start()

    def chunk_copy(b, k):
        rows = pl.ds(k * cr, cr)
        return pltpu.make_async_remote_copy(
            src_ref=o_buf.at[b, rows],
            dst_ref=z_buf.at[b, pl.ds(k * cr + 1, cr)],
            send_sem=csend.at[b, k],
            recv_sem=crecv.at[b, k],
            device_id=(g + 1, s),
            device_id_type=MESH,
        )

    def edge_copy(b, low):
        src, dst, to = (0, sr + 1, s - 1) if low else (sr - 1, 0, s + 1)
        i = 0 if low else 1
        return pltpu.make_async_remote_copy(
            src_ref=o_buf.at[b, pl.ds(src, 1)],
            dst_ref=z_buf.at[b, pl.ds(dst, 1)],
            send_sem=esend.at[b, i],
            recv_sem=erecv.at[b, i],
            device_id=(g + 1, to),
            device_id_type=MESH,
        )

    def out_copy(b, k):
        rows = pl.ds(k * cr, cr)
        return pltpu.make_async_copy(
            o_buf.at[b, rows], out.at[0, b, rows], osem.at[b, k]
        )

    span = cr * cols
    width = 256

    def order(p):
        return jnp.where(p == n - 1, n - 1, jnp.where(p == n - 2, 0, p + 1))

    def section(b, p):
        k = order(p)

        @pl.when(g > 0)
        def _():
            @pl.when(p == 0)
            def _():
                for j in range(3):
                    chunk_copy(b, j).wait_recv()

            @pl.when((p > 0) & (p < n - 2))
            def _():
                chunk_copy(b, p + 2).wait_recv()

        @pl.when((p == n - 2) & (s > 0))
        def _():
            edge_copy(b, False).wait_recv()

        @pl.when((p == n - 1) & (s < N - 1))
        def _():
            edge_copy(b, True).wait_recv()

        data = jnp.concatenate(
            [z_buf[b, pl.ds(k * cr + a, cr)].reshape(span, K2) for a in range(3)],
            axis=1,
        )
        place = lax.broadcasted_iota(jnp.int32, (cr, cols, width), 1).reshape(span, width)
        for q in range(K2 // width):
            part = [
                jnp.dot(
                    data,
                    wsec_v[:, c * K2 + q * width : c * K2 + (q + 1) * width],
                    preferred_element_type=jnp.float32,
                )
                for c in range(3)
            ]
            left = jnp.where(place == 0, 0.0, pltpu.roll(part[0], 1, 0))
            right = jnp.where(place == cols - 1, 0.0, pltpu.roll(part[2], span - 1, 0))
            inner = z_buf[
                b, pl.ds(k * cr + 1, cr), :, q * width : (q + 1) * width
            ].reshape(span, width)
            value = jnp.maximum(inner.astype(jnp.float32) + left + part[1] + right, 0.0)
            o_buf[b, pl.ds(k * cr, cr), :, q * width : (q + 1) * width] = value.astype(
                jnp.bfloat16
            ).reshape(cr, cols, width)
        out_copy(b, k).start()

        @pl.when(g < S - 1)
        def _():
            @pl.when((k == 0) & (s > 0))
            def _():
                edge_copy(b, True).start()

            @pl.when((k == n - 1) & (s < N - 1))
            def _():
                edge_copy(b, False).start()

            @pl.when(p >= 2)
            def _():
                chunk_copy(b, order(p - 2)).wait_send()

            if b > 0:

                @pl.when(p < 2)
                def _():
                    chunk_copy(b - 1, order(p + n - 2)).wait_send()

            chunk_copy(b, k).start()

    for b in range(B):

        @pl.when(g == 0)
        def _():
            arrive(b)

        def step(p, carry):
            section(b, p)
            return carry

        lax.fori_loop(0, n, step, 0)

    for b in range(B):
        for i, (dg, ds) in enumerate(DIRS):

            @pl.when(inside(g + dg, s + ds))
            def _():
                border(b, i).wait_send()

        if b == B - 1:
            for away, home, remote, local in pieces(b):

                @pl.when(away)
                def _():
                    remote().wait_send()

        @pl.when((g == 0) & (s > 0))
        def _():
            strip_copy(b, True).wait_send()

        @pl.when((g == 0) & (s < N - 1))
        def _():
            strip_copy(b, False).wait_send()

        @pl.when(g < S - 1)
        def _():
            @pl.when(s > 0)
            def _():
                edge_copy(b, True).wait_send()

            @pl.when(s < N - 1)
            def _():
                edge_copy(b, False).wait_send()

            if b == B - 1:
                chunk_copy(b, 0).wait_send()
                chunk_copy(b, n - 1).wait_send()

        for k in range(n):
            out_copy(b, k).wait()


def shards(S, N, features, weight_first, weight_second, weight_down, section_weights):
    B, R, C, K1 = features.shape
    K2 = weight_down.shape[3]
    RD, CD = R // 2, C // 2
    m = N // S
    sr = RD // m
    cols = CD * N
    n = sr // max(1, 256 // cols)
    pitch = R + EDGE
    bf16, f32 = jnp.bfloat16, jnp.float32
    dma = pltpu.SemaphoreType.DMA
    anywhere = pl.BlockSpec(memory_space=pl.ANY)
    flops = 2 * B * (R * C * 18 * K1 * K1 + RD * CD * 4 * K1 * K2 + sr * cols * 9 * K2 * K2)
    return pl.pallas_call(
        functools.partial(kernel, (S, N, B, R, C, K1, K2)),
        out_shape=jax.ShapeDtypeStruct((1, B, sr, cols, K2), bf16),
        in_specs=[pl.BlockSpec(memory_space=pltpu.HBM)] * 5,
        out_specs=anywhere,
        scratch_shapes=[
            pltpu.VMEM((B, R, C, K1), bf16),
            pltpu.VMEM((B, C + 4, EDGE, K1), bf16),
            pltpu.VMEM((B, C + 4, EDGE, K1), bf16),
            pltpu.VMEM((B, C + 4, pitch, K1), bf16),
            pltpu.VMEM((C + 2, pitch, K1), bf16),
            pltpu.VMEM((K1 // 128, C * R, 128), f32),
            pltpu.VMEM((B, RD * CD, K2), bf16),
            pltpu.VMEM((B, N, sr * CD, K2), bf16),
            pltpu.VMEM((B, sr + 2, cols, K2), bf16),
            pltpu.VMEM((B, sr, cols, K2), bf16),
            pltpu.VMEM((3 * K1, 3 * K1), bf16),
            pltpu.VMEM((3 * K1, 3 * K1), bf16),
            pltpu.VMEM((4 * K1, K2), bf16),
            pltpu.VMEM((3 * K2, 3 * K2), bf16),
            dma((31,)),
            dma((B,)),
            dma((B, 8)),
            dma((B, 8)),
            dma((B, m)),
            dma((B, N)),
            dma((B, n)),
            dma((B, n)),
            dma((B, 2)),
            dma((B, 2)),
            dma((B, 2)),
            dma((B, n)),
        ],
        compiler_params=pltpu.CompilerParams(
            collective_id=0, has_side_effects=True, vmem_limit_bytes=56 * 1024 * 1024
        ),
        cost_estimate=pl.CostEstimate(
            flops=flops, bytes_accessed=16 * 1024 * 1024, transcendentals=0
        ),
    )(
        features,
        weight_first,
        weight_second,
        weight_down,
        section_weights,
    )


def solution(mesh):
    return jax.shard_map(
        functools.partial(shards, mesh.shape["segment"], mesh.shape["strip"]),
        mesh=mesh,
        in_specs=(
            P(None, "segment", "strip", None),
            P(),
            P(),
            P(),
            P("segment", None, None, None, None),
        ),
        out_specs=P("segment", None, "strip", None, None),
        check_vma=False,
    )
```

```python
import functools

import jax
import jax.numpy as jnp
from jax import lax
from jax.experimental import pallas as pl
from jax.experimental.pallas import tpu as pltpu
from jax.sharding import PartitionSpec as P

MESH = pl.DeviceIdType.MESH
EDGE = 16
DIRS = [(dg, ds) for dg in (-1, 0, 1) for ds in (-1, 0, 1) if (dg, ds) != (0, 0)]


def fits(count, pitch, limit):
    best = 1
    for size in range(1, count + 1):
        if count % size == 0 and size * pitch <= limit:
            best = size
    return best


def kernel(
    dims,
    feat,
    wf,
    ws,
    wd,
    wsec,
    out,
    raw_buf,
    top_buf,
    bot_buf,
    x_buf,
    f_buf,
    s_buf,
    d_buf,
    r_buf,
    z_buf,
    o_buf,
    wf_v,
    ws_v,
    wd_v,
    wsec_v,
    wsem,
    fsem,
    hsend,
    hrecv,
    rsend,
    rmain,
    csend,
    crecv,
    zsend,
    esend,
    erecv,
    osem,
):
    S, N, B, R, C, K1, K2 = dims
    RD, CD = R // 2, C // 2
    m = N // S
    sr = RD // m
    cols = CD * N
    cr = max(1, 256 // cols)
    n = sr // cr
    pitch = R + EDGE
    g = lax.axis_index("segment")
    s = lax.axis_index("strip")

    copies = []
    for a in range(3):
        for c in range(3):
            copies.append(
                (0, wf.at[a, c], wf_v.at[pl.ds(c * K1, K1), pl.ds(a * K1, K1)])
            )
    for a in range(3):
        for c in range(3):
            copies.append(
                (1, ws.at[a, c], ws_v.at[pl.ds(c * K1, K1), pl.ds(a * K1, K1)])
            )
    for a in range(2):
        for c in range(2):
            copies.append((2, wd.at[a, c], wd_v.at[pl.ds((2 * a + c) * K1, K1)]))
    for a in range(3):
        for c in range(3):
            copies.append(
                (3, wsec.at[0, a, c], wsec_v.at[pl.ds(a * K2, K2), pl.ds(c * K2, K2)])
            )
    weights = [
        (group, pltpu.make_async_copy(src, dst, wsem.at[i]))
        for i, (group, src, dst) in enumerate(copies)
    ]

    def weights_wait(which):
        for group, copy in weights:
            if group == which:
                copy.wait()

    centre = [
        pltpu.make_async_copy(
            feat.at[b], raw_buf.at[b], fsem.at[b]
        )
        for b in range(B)
    ]
    for copy in centre:
        copy.start()
    for _, copy in weights:
        copy.start()

    zero = jnp.bfloat16(0)
    x_buf[:, 0:2] = jnp.full((B, 2, pitch, K1), zero)
    x_buf[:, C + 2 : C + 4] = jnp.full((B, 2, pitch, K1), zero)
    top_buf[...] = jnp.full((B, C + 4, EDGE, K1), zero)
    bot_buf[...] = jnp.full((B, C + 4, EDGE, K1), zero)
    z_buf[:, 0] = jnp.full((B, cols, K2), zero)
    z_buf[:, sr + 1] = jnp.full((B, cols, K2), zero)

    def inside(gg, ss):
        return (gg >= 0) & (gg < S) & (ss >= 0) & (ss < N)

    barrier = pltpu.get_barrier_semaphore()
    due = jnp.int32(0)
    partners = [(g + dg, s + ds, inside(g + dg, s + ds)) for dg, ds in DIRS]
    for k in range(m):
        strip = g * m + k
        partners.append((jnp.int32(0), strip, ~((g == 0) & (s == strip))))
    for src in range(N):
        band = lax.div(s, m)
        away = ~((band == 0) & (s == src))
        partners.append((band, jnp.int32(src), (g == 0) & away))
    for gg, ss, there in partners:
        due = due + jnp.where(there, 1, 0)

        @pl.when(there)
        def _():
            pl.semaphore_signal(
                barrier, inc=1, device_id=(gg, ss), device_id_type=MESH
            )

    def swap(outer, inner):
        shape = (inner, outer, outer * inner)
        i, j, q = [lax.broadcasted_iota(jnp.int32, shape, d) for d in range(3)]
        hot = jnp.where(q == j * inner + i, 1.0, 0.0)
        return hot.reshape(outer * inner, outer * inner).astype(jnp.bfloat16)

    turn = swap(EDGE, C)
    for b in range(B):
        centre[b].wait()
        for q in range(R // EDGE):
            block = raw_buf[b, q * EDGE : (q + 1) * EDGE].reshape(EDGE * C, K1)
            block = jnp.dot(turn, block, preferred_element_type=jnp.float32)
            x_buf[b, 2 : C + 2, q * EDGE : (q + 1) * EDGE] = block.astype(
                jnp.bfloat16
            ).reshape(C, EDGE, K1)

    pl.semaphore_wait(barrier, due)

    row_src = {-1: (0, EDGE), 0: (0, R), 1: (R - EDGE, EDGE)}
    col_src = {-1: (2, 2), 0: (2, C), 1: (C, 2)}
    col_dst = {-1: C + 2, 0: 2, 1: 0}

    def border(b, i):
        dg, ds = DIRS[i]
        r0, rn = row_src[dg]
        c0, cn = col_src[ds]
        where = pl.ds(col_dst[ds], cn)
        if dg == 0:
            dst = x_buf.at[b, where, pl.ds(0, R)]
        else:
            dst = (top_buf if dg == 1 else bot_buf).at[b, where]
        return pltpu.make_async_remote_copy(
            src_ref=x_buf.at[b, pl.ds(c0, cn), pl.ds(r0, rn)],
            dst_ref=dst,
            send_sem=hsend.at[b, i],
            recv_sem=hrecv.at[b, i],
            device_id=(g + dg, s + ds),
            device_id_type=MESH,
        )

    for b in range(B):
        for i, (dg, ds) in enumerate(DIRS):

            @pl.when(inside(g + dg, s + ds))
            def _():
                border(b, i).start()

    def pieces(b):
        made = []
        for k in range(m):
            strip = g * m + k
            src = d_buf.at[b, pl.ds(k * sr * CD, sr * CD)]
            dst = r_buf.at[b, s]
            remote = functools.partial(
                pltpu.make_async_remote_copy,
                src_ref=src,
                dst_ref=dst,
                send_sem=rsend.at[b, k],
                recv_sem=rmain.at[b, s],
                device_id=(0, strip),
                device_id_type=MESH,
            )
            local = functools.partial(pltpu.make_async_copy, src, dst, rmain.at[b, s])
            own = (g == 0) & (s == strip)
            made.append((~own, own, remote, local))
        return made

    def conv_rows(buf, first_col, size, weight, sel):
        data = [
            buf[sel(first_col + j, size)].reshape(size * pitch, K1) for j in range(3)
        ]
        data = jnp.concatenate(data, axis=1)
        part = [
            jnp.dot(
                data,
                weight[:, a * K1 : (a + 1) * K1],
                preferred_element_type=jnp.float32,
            )
            for a in range(3)
        ]
        part = [p.reshape(size, pitch, K1) for p in part]
        return pltpu.roll(part[0], 1, 1) + part[1] + pltpu.roll(part[2], pitch - 1, 1)

    size1 = fits(C + 2, pitch, 480)
    size2 = fits(C, pitch, 640)

    def stem(b):
        for i, (dg, ds) in enumerate(DIRS):

            @pl.when(inside(g - dg, s - ds))
            def _():
                border(b, i).wait_recv()

        low = lax.broadcasted_iota(jnp.int32, (C + 4, EDGE, K1), 1) < EDGE // 2
        x_buf[b, :, R:] = jnp.where(
            low, bot_buf[b].astype(jnp.float32), top_buf[b].astype(jnp.float32)
        ).astype(jnp.bfloat16)
        if b == 0:
            weights_wait(0)

        def one(t, carry):
            c0 = t * size1
            conv = conv_rows(
                x_buf, c0, size1, wf_v, lambda at, size: (b, pl.ds(at, size))
            )
            inner = x_buf[b, pl.ds(c0 + 1, size1)].astype(jnp.float32)
            value = jnp.maximum(inner + conv, 0.0)
            col = lax.broadcasted_iota(jnp.int32, (size1, pitch, K1), 0) + (
                s * C + c0 - 1
            )
            row = lax.broadcasted_iota(jnp.int32, (size1, pitch, K1), 1)
            row = jnp.where(row < R + EDGE // 2, row, row - pitch) + g * R
            keep = (col >= 0) & (col < N * C) & (row >= 0) & (row < S * R)
            f_buf[pl.ds(c0, size1)] = jnp.where(keep, value, 0.0).astype(jnp.bfloat16)
            return carry

        lax.fori_loop(0, (C + 2) // size1, one, 0)
        if b == 0:
            weights_wait(1)

        def two(t, carry):
            c0 = t * size2
            conv = conv_rows(f_buf, c0, size2, ws_v, lambda at, size: (pl.ds(at, size),))
            conv = conv[:, :R]
            inner = f_buf[pl.ds(c0 + 1, size2), :R].astype(jnp.float32)
            value = jnp.maximum(inner + conv, 0.0)
            at = pl.multiple_of(c0 * R, R)
            value = value.reshape(size2 * R, K1)
            for q in range(K1 // 128):
                s_buf[q, pl.ds(at, size2 * R), :] = value[:, q * 128 : (q + 1) * 128]
            return carry

        lax.fori_loop(0, C // size2, two, 0)
        if b == 0:
            weights_wait(2)
        taps = []
        for a in range(2):
            picked = jnp.concatenate(
                [
                    s_buf[q, pl.ds(a, C * RD, stride=2), :]
                    for q in range(K1 // 128)
                ],
                axis=1,
            )
            picked = picked.reshape(CD, 2, RD, K1)
            for c in range(2):
                taps.append(picked[:, c].reshape(CD * RD, K1).astype(jnp.bfloat16))
        reduced = jnp.dot(
            jnp.concatenate(taps, axis=1), wd_v[...], preferred_element_type=jnp.float32
        )
        reduced = jnp.maximum(reduced, 0.0).astype(jnp.bfloat16)
        d_buf[b] = jnp.dot(
            swap(CD, RD), reduced, preferred_element_type=jnp.float32
        ).astype(jnp.bfloat16)
        if b > 0:
            for away, home, remote, local in pieces(b - 1):

                @pl.when(away)
                def _():
                    remote().wait_send()

        for away, home, remote, local in pieces(b):

            @pl.when(away)
            def _():
                remote().start()

            @pl.when(home)
            def _():
                local().start()

    for b in range(B):
        stem(b)
    weights_wait(3)

    def strip_copy(b, low):
        src, dst, to = (1, sr + 1, s - 1) if low else (sr, 0, s + 1)
        i = 0 if low else 1
        return pltpu.make_async_remote_copy(
            src_ref=z_buf.at[b, pl.ds(src, 1)],
            dst_ref=z_buf.at[b, pl.ds(dst, 1)],
            send_sem=zsend.at[b, i],
            recv_sem=erecv.at[b, i],
            device_id=(g, to),
            device_id_type=MESH,
        )

    def arrive(b):
        def waits(src, carry):
            part = r_buf.at[b, src]
            pltpu.make_async_copy(part, part, rmain.at[b, src]).wait()
            return carry

        lax.fori_loop(0, N, waits, 0)
        group = max(1, EDGE // CD)
        for q in range(N // group):
            parts = [
                r_buf[b, q * group + j].astype(jnp.float32).reshape(sr, CD, K2)
                for j in range(group)
            ]
            whole = parts[0] if group == 1 else jnp.concatenate(parts, axis=1)
            z_buf[b, 1 : sr + 1, q * group * CD : (q + 1) * group * CD] = whole.astype(
                jnp.bfloat16
            )

        @pl.when(s > 0)
        def _():
            strip_copy(b, True).start()

        @pl.when(s < N - 1)
        def _():
            strip_copy(b, False).start()

    def chunk_copy(b, k):
        rows = pl.ds(k * cr, cr)
        return pltpu.make_async_remote_copy(
            src_ref=o_buf.at[b, rows],
            dst_ref=z_buf.at[b, pl.ds(k * cr + 1, cr)],
            send_sem=csend.at[b, k],
            recv_sem=crecv.at[b, k],
            device_id=(g + 1, s),
            device_id_type=MESH,
        )

    def edge_copy(b, low):
        src, dst, to = (0, sr + 1, s - 1) if low else (sr - 1, 0, s + 1)
        i = 0 if low else 1
        return pltpu.make_async_remote_copy(
            src_ref=o_buf.at[b, pl.ds(src, 1)],
            dst_ref=z_buf.at[b, pl.ds(dst, 1)],
            send_sem=esend.at[b, i],
            recv_sem=erecv.at[b, i],
            device_id=(g + 1, to),
            device_id_type=MESH,
        )

    def out_copy(b, k):
        rows = pl.ds(k * cr, cr)
        return pltpu.make_async_copy(
            o_buf.at[b, rows], out.at[0, b, rows], osem.at[b, k]
        )

    span = cr * cols
    width = 256

    def order(p):
        return jnp.where(p == n - 1, n - 1, jnp.where(p == n - 2, 0, p + 1))

    def section(b, p):
        k = order(p)

        @pl.when(g > 0)
        def _():
            @pl.when(p == 0)
            def _():
                for j in range(3):
                    chunk_copy(b, j).wait_recv()

            @pl.when((p > 0) & (p < n - 2))
            def _():
                chunk_copy(b, p + 2).wait_recv()

        @pl.when((p == n - 2) & (s > 0))
        def _():
            edge_copy(b, False).wait_recv()

        @pl.when((p == n - 1) & (s < N - 1))
        def _():
            edge_copy(b, True).wait_recv()

        data = jnp.concatenate(
            [z_buf[b, pl.ds(k * cr + a, cr)].reshape(span, K2) for a in range(3)],
            axis=1,
        )
        place = lax.broadcasted_iota(jnp.int32, (cr, cols, width), 1).reshape(span, width)
        for q in range(K2 // width):
            part = [
                jnp.dot(
                    data,
                    wsec_v[:, c * K2 + q * width : c * K2 + (q + 1) * width],
                    preferred_element_type=jnp.float32,
                )
                for c in range(3)
            ]
            left = jnp.where(place == 0, 0.0, pltpu.roll(part[0], 1, 0))
            right = jnp.where(place == cols - 1, 0.0, pltpu.roll(part[2], span - 1, 0))
            inner = z_buf[
                b, pl.ds(k * cr + 1, cr), :, q * width : (q + 1) * width
            ].reshape(span, width)
            value = jnp.maximum(inner.astype(jnp.float32) + left + part[1] + right, 0.0)
            o_buf[b, pl.ds(k * cr, cr), :, q * width : (q + 1) * width] = value.astype(
                jnp.bfloat16
            ).reshape(cr, cols, width)
        out_copy(b, k).start()

        @pl.when(g < S - 1)
        def _():
            @pl.when((k == 0) & (s > 0))
            def _():
                edge_copy(b, True).start()

            @pl.when((k == n - 1) & (s < N - 1))
            def _():
                edge_copy(b, False).start()

            @pl.when(p >= 2)
            def _():
                chunk_copy(b, order(p - 2)).wait_send()

            if b > 0:

                @pl.when(p < 2)
                def _():
                    chunk_copy(b - 1, order(p + n - 2)).wait_send()

            chunk_copy(b, k).start()

    for b in range(B):

        @pl.when(g == 0)
        def _():
            arrive(b)

        def step(p, carry):
            section(b, p)
            return carry

        lax.fori_loop(0, n, step, 0)

    for b in range(B):
        for i, (dg, ds) in enumerate(DIRS):

            @pl.when(inside(g + dg, s + ds))
            def _():
                border(b, i).wait_send()

        if b == B - 1:
            for away, home, remote, local in pieces(b):

                @pl.when(away)
                def _():
                    remote().wait_send()

        @pl.when((g == 0) & (s > 0))
        def _():
            strip_copy(b, True).wait_send()

        @pl.when((g == 0) & (s < N - 1))
        def _():
            strip_copy(b, False).wait_send()

        @pl.when(g < S - 1)
        def _():
            @pl.when(s > 0)
            def _():
                edge_copy(b, True).wait_send()

            @pl.when(s < N - 1)
            def _():
                edge_copy(b, False).wait_send()

            if b == B - 1:
                chunk_copy(b, 0).wait_send()
                chunk_copy(b, n - 1).wait_send()

        for k in range(n):
            out_copy(b, k).wait()


def shards(S, N, features, weight_first, weight_second, weight_down, section_weights):
    B, R, C, K1 = features.shape
    K2 = weight_down.shape[3]
    RD, CD = R // 2, C // 2
    m = N // S
    sr = RD // m
    cols = CD * N
    n = sr // max(1, 256 // cols)
    pitch = R + EDGE
    bf16, f32 = jnp.bfloat16, jnp.float32
    dma = pltpu.SemaphoreType.DMA
    anywhere = pl.BlockSpec(memory_space=pl.ANY)
    flops = 2 * B * (R * C * 18 * K1 * K1 + RD * CD * 4 * K1 * K2 + sr * cols * 9 * K2 * K2)
    return pl.pallas_call(
        functools.partial(kernel, (S, N, B, R, C, K1, K2)),
        out_shape=jax.ShapeDtypeStruct((1, B, sr, cols, K2), bf16),
        in_specs=[pl.BlockSpec(memory_space=pltpu.HBM)] * 5,
        out_specs=anywhere,
        scratch_shapes=[
            pltpu.VMEM((B, R, C, K1), bf16),
            pltpu.VMEM((B, C + 4, EDGE, K1), bf16),
            pltpu.VMEM((B, C + 4, EDGE, K1), bf16),
            pltpu.VMEM((B, C + 4, pitch, K1), bf16),
            pltpu.VMEM((C + 2, pitch, K1), bf16),
            pltpu.VMEM((K1 // 128, C * R, 128), f32),
            pltpu.VMEM((B, RD * CD, K2), bf16),
            pltpu.VMEM((B, N, sr * CD, K2), bf16),
            pltpu.VMEM((B, sr + 2, cols, K2), bf16),
            pltpu.VMEM((B, sr, cols, K2), bf16),
            pltpu.VMEM((3 * K1, 3 * K1), bf16),
            pltpu.VMEM((3 * K1, 3 * K1), bf16),
            pltpu.VMEM((4 * K1, K2), bf16),
            pltpu.VMEM((3 * K2, 3 * K2), bf16),
            dma((31,)),
            dma((B,)),
            dma((B, 8)),
            dma((B, 8)),
            dma((B, m)),
            dma((B, N)),
            dma((B, n)),
            dma((B, n)),
            dma((B, 2)),
            dma((B, 2)),
            dma((B, 2)),
            dma((B, n)),
        ],
        compiler_params=pltpu.CompilerParams(
            collective_id=0, has_side_effects=True, vmem_limit_bytes=56 * 1024 * 1024
        ),
        cost_estimate=pl.CostEstimate(
            flops=flops, bytes_accessed=16 * 1024 * 1024, transcendentals=0
        ),
    )(
        features,
        weight_first,
        weight_second,
        weight_down,
        section_weights,
    )


def solution(mesh):
    return jax.shard_map(
        functools.partial(shards, mesh.shape["segment"], mesh.shape["strip"]),
        mesh=mesh,
        in_specs=(
            P(None, "segment", "strip", None),
            P(),
            P(),
            P(),
            P("segment", None, None, None, None),
        ),
        out_specs=P("segment", None, "strip", None, None),
        check_vma=False,
    )
```

```python
import functools

import jax
import jax.numpy as jnp
from jax import lax
from jax.experimental import pallas as pl
from jax.experimental.pallas import tpu as pltpu
from jax.sharding import PartitionSpec as P

MESH = pl.DeviceIdType.MESH
EDGE = 16
DIRS = [(dg, ds) for dg in (-1, 0, 1) for ds in (-1, 0, 1) if (dg, ds) != (0, 0)]


def fits(count, pitch, limit):
    best = 1
    for size in range(1, count + 1):
        if count % size == 0 and size * pitch <= limit:
            best = size
    return best


def kernel(
    dims,
    feat,
    wf,
    ws,
    wd,
    wsec,
    out,
    raw_buf,
    top_buf,
    bot_buf,
    x_buf,
    f_buf,
    s_buf,
    d_buf,
    r_buf,
    z_buf,
    o_buf,
    wf_v,
    ws_v,
    wd_v,
    wsec_v,
    wsem,
    fsem,
    hsend,
    hrecv,
    rsend,
    rmain,
    csend,
    crecv,
    zsend,
    esend,
    erecv,
    osem,
):
    S, N, B, R, C, K1, K2 = dims
    RD, CD = R // 2, C // 2
    m = N // S
    sr = RD // m
    cols = CD * N
    cr = max(1, 256 // cols)
    n = sr // cr
    pitch = R + EDGE
    g = lax.axis_index("segment")
    s = lax.axis_index("strip")

    copies = []
    for a in range(3):
        for c in range(3):
            copies.append(
                (0, wf.at[a, c], wf_v.at[pl.ds(c * K1, K1), pl.ds(a * K1, K1)])
            )
    for a in range(3):
        for c in range(3):
            copies.append(
                (1, ws.at[a, c], ws_v.at[pl.ds(c * K1, K1), pl.ds(a * K1, K1)])
            )
    for a in range(2):
        for c in range(2):
            copies.append((2, wd.at[a, c], wd_v.at[pl.ds((2 * a + c) * K1, K1)]))
    for a in range(3):
        for c in range(3):
            copies.append(
                (3, wsec.at[0, a, c], wsec_v.at[pl.ds(a * K2, K2), pl.ds(c * K2, K2)])
            )
    weights = [
        (group, pltpu.make_async_copy(src, dst, wsem.at[i]))
        for i, (group, src, dst) in enumerate(copies)
    ]

    def weights_wait(which):
        for group, copy in weights:
            if group == which:
                copy.wait()

    centre = [
        pltpu.make_async_copy(
            feat.at[b], raw_buf.at[b], fsem.at[b]
        )
        for b in range(B)
    ]
    for copy in centre:
        copy.start()
    for _, copy in weights:
        copy.start()

    zero = jnp.bfloat16(0)
    x_buf[:, 0:2] = jnp.full((B, 2, pitch, K1), zero)
    x_buf[:, C + 2 : C + 4] = jnp.full((B, 2, pitch, K1), zero)
    top_buf[...] = jnp.full((B, C + 4, EDGE, K1), zero)
    bot_buf[...] = jnp.full((B, C + 4, EDGE, K1), zero)
    z_buf[:, 0] = jnp.full((B, cols, K2), zero)
    z_buf[:, sr + 1] = jnp.full((B, cols, K2), zero)

    def inside(gg, ss):
        return (gg >= 0) & (gg < S) & (ss >= 0) & (ss < N)

    barrier = pltpu.get_barrier_semaphore()
    due = jnp.int32(0)
    partners = [(g + dg, s + ds, inside(g + dg, s + ds)) for dg, ds in DIRS]
    for k in range(m):
        strip = g * m + k
        partners.append((jnp.int32(0), strip, ~((g == 0) & (s == strip))))
    for src in range(N):
        band = lax.div(s, m)
        away = ~((band == 0) & (s == src))
        partners.append((band, jnp.int32(src), (g == 0) & away))
    for gg, ss, there in partners:
        due = due + jnp.where(there, 1, 0)

        @pl.when(there)
        def _():
            pl.semaphore_signal(
                barrier, inc=1, device_id=(gg, ss), device_id_type=MESH
            )

    def swap(outer, inner):
        shape = (inner, outer, outer * inner)
        i, j, q = [lax.broadcasted_iota(jnp.int32, shape, d) for d in range(3)]
        hot = jnp.where(q == j * inner + i, 1.0, 0.0)
        return hot.reshape(outer * inner, outer * inner).astype(jnp.bfloat16)

    turn = swap(EDGE, C)
    for b in range(B):
        centre[b].wait()
        for q in range(R // EDGE):
            block = raw_buf[b, q * EDGE : (q + 1) * EDGE].reshape(EDGE * C, K1)
            block = jnp.dot(turn, block, preferred_element_type=jnp.float32)
            x_buf[b, 2 : C + 2, q * EDGE : (q + 1) * EDGE] = block.astype(
                jnp.bfloat16
            ).reshape(C, EDGE, K1)

    pl.semaphore_wait(barrier, due)

    row_src = {-1: (0, EDGE), 0: (0, R), 1: (R - EDGE, EDGE)}
    col_src = {-1: (2, 2), 0: (2, C), 1: (C, 2)}
    col_dst = {-1: C + 2, 0: 2, 1: 0}

    def border(b, i):
        dg, ds = DIRS[i]
        r0, rn = row_src[dg]
        c0, cn = col_src[ds]
        where = pl.ds(col_dst[ds], cn)
        if dg == 0:
            dst = x_buf.at[b, where, pl.ds(0, R)]
        else:
            dst = (top_buf if dg == 1 else bot_buf).at[b, where]
        return pltpu.make_async_remote_copy(
            src_ref=x_buf.at[b, pl.ds(c0, cn), pl.ds(r0, rn)],
            dst_ref=dst,
            send_sem=hsend.at[b, i],
            recv_sem=hrecv.at[b, i],
            device_id=(g + dg, s + ds),
            device_id_type=MESH,
        )

    for b in range(B):
        for i, (dg, ds) in enumerate(DIRS):

            @pl.when(inside(g + dg, s + ds))
            def _():
                border(b, i).start()

    def pieces(b):
        made = []
        for k in range(m):
            strip = g * m + k
            src = d_buf.at[b, pl.ds(k * sr * CD, sr * CD)]
            dst = r_buf.at[b, s]
            remote = functools.partial(
                pltpu.make_async_remote_copy,
                src_ref=src,
                dst_ref=dst,
                send_sem=rsend.at[b, k],
                recv_sem=rmain.at[b, s],
                device_id=(0, strip),
                device_id_type=MESH,
            )
            local = functools.partial(pltpu.make_async_copy, src, dst, rmain.at[b, s])
            own = (g == 0) & (s == strip)
            made.append((~own, own, remote, local))
        return made

    def conv_rows(buf, first_col, size, weight, sel):
        data = [
            buf[sel(first_col + j, size)].reshape(size * pitch, K1) for j in range(3)
        ]
        data = jnp.concatenate(data, axis=1)
        part = [
            jnp.dot(
                data,
                weight[:, a * K1 : (a + 1) * K1],
                preferred_element_type=jnp.float32,
            )
            for a in range(3)
        ]
        part = [p.reshape(size, pitch, K1) for p in part]
        return pltpu.roll(part[0], 1, 1) + part[1] + pltpu.roll(part[2], pitch - 1, 1)

    size1 = fits(C + 2, pitch, 480)
    size2 = fits(C, pitch, 640)

    def stem(b):
        for i, (dg, ds) in enumerate(DIRS):

            @pl.when(inside(g - dg, s - ds))
            def _():
                border(b, i).wait_recv()

        low = lax.broadcasted_iota(jnp.int32, (C + 4, EDGE, K1), 1) < EDGE // 2
        x_buf[b, :, R:] = jnp.where(
            low, bot_buf[b].astype(jnp.float32), top_buf[b].astype(jnp.float32)
        ).astype(jnp.bfloat16)
        if b == 0:
            weights_wait(0)

        def one(t, carry):
            c0 = t * size1
            conv = conv_rows(
                x_buf, c0, size1, wf_v, lambda at, size: (b, pl.ds(at, size))
            )
            inner = x_buf[b, pl.ds(c0 + 1, size1)].astype(jnp.float32)
            value = jnp.maximum(inner + conv, 0.0)
            col = lax.broadcasted_iota(jnp.int32, (size1, pitch, K1), 0) + (
                s * C + c0 - 1
            )
            row = lax.broadcasted_iota(jnp.int32, (size1, pitch, K1), 1)
            row = jnp.where(row < R + EDGE // 2, row, row - pitch) + g * R
            keep = (col >= 0) & (col < N * C) & (row >= 0) & (row < S * R)
            f_buf[pl.ds(c0, size1)] = jnp.where(keep, value, 0.0).astype(jnp.bfloat16)
            return carry

        lax.fori_loop(0, (C + 2) // size1, one, 0)
        if b == 0:
            weights_wait(1)

        def two(t, carry):
            c0 = t * size2
            conv = conv_rows(f_buf, c0, size2, ws_v, lambda at, size: (pl.ds(at, size),))
            conv = conv[:, :R]
            inner = f_buf[pl.ds(c0 + 1, size2), :R].astype(jnp.float32)
            value = jnp.maximum(inner + conv, 0.0)
            at = pl.multiple_of(c0 * R, R)
            value = value.reshape(size2 * R, K1)
            for q in range(K1 // 128):
                s_buf[q, pl.ds(at, size2 * R), :] = value[:, q * 128 : (q + 1) * 128]
            return carry

        lax.fori_loop(0, C // size2, two, 0)
        if b == 0:
            weights_wait(2)
        taps = []
        for a in range(2):
            picked = jnp.concatenate(
                [
                    s_buf[q, pl.ds(a, C * RD, stride=2), :]
                    for q in range(K1 // 128)
                ],
                axis=1,
            )
            picked = picked.reshape(CD, 2, RD, K1)
            for c in range(2):
                taps.append(picked[:, c].reshape(CD * RD, K1).astype(jnp.bfloat16))
        reduced = jnp.dot(
            jnp.concatenate(taps, axis=1), wd_v[...], preferred_element_type=jnp.float32
        )
        reduced = jnp.maximum(reduced, 0.0).astype(jnp.bfloat16)
        d_buf[b] = jnp.dot(
            swap(CD, RD), reduced, preferred_element_type=jnp.float32
        ).astype(jnp.bfloat16)
        if b > 0:
            for away, home, remote, local in pieces(b - 1):

                @pl.when(away)
                def _():
                    remote().wait_send()

        for away, home, remote, local in pieces(b):

            @pl.when(away)
            def _():
                remote().start()

            @pl.when(home)
            def _():
                local().start()

    for b in range(B):
        stem(b)
    weights_wait(3)

    def strip_copy(b, low):
        src, dst, to = (1, sr + 1, s - 1) if low else (sr, 0, s + 1)
        i = 0 if low else 1
        return pltpu.make_async_remote_copy(
            src_ref=z_buf.at[b, pl.ds(src, 1)],
            dst_ref=z_buf.at[b, pl.ds(dst, 1)],
            send_sem=zsend.at[b, i],
            recv_sem=erecv.at[b, i],
            device_id=(g, to),
            device_id_type=MESH,
        )

    def arrive(b):
        def waits(src, carry):
            part = r_buf.at[b, src]
            pltpu.make_async_copy(part, part, rmain.at[b, src]).wait()
            return carry

        lax.fori_loop(0, N, waits, 0)
        group = max(1, EDGE // CD)
        for q in range(N // group):
            parts = [
                r_buf[b, q * group + j].astype(jnp.float32).reshape(sr, CD, K2)
                for j in range(group)
            ]
            whole = parts[0] if group == 1 else jnp.concatenate(parts, axis=1)
            z_buf[b, 1 : sr + 1, q * group * CD : (q + 1) * group * CD] = whole.astype(
                jnp.bfloat16
            )

        @pl.when(s > 0)
        def _():
            strip_copy(b, True).start()

        @pl.when(s < N - 1)
        def _():
            strip_copy(b, False).start()

    def chunk_copy(b, k):
        rows = pl.ds(k * cr, cr)
        return pltpu.make_async_remote_copy(
            src_ref=o_buf.at[b, rows],
            dst_ref=z_buf.at[b, pl.ds(k * cr + 1, cr)],
            send_sem=csend.at[b, k],
            recv_sem=crecv.at[b, k],
            device_id=(g + 1, s),
            device_id_type=MESH,
        )

    def edge_copy(b, low):
        src, dst, to = (0, sr + 1, s - 1) if low else (sr - 1, 0, s + 1)
        i = 0 if low else 1
        return pltpu.make_async_remote_copy(
            src_ref=o_buf.at[b, pl.ds(src, 1)],
            dst_ref=z_buf.at[b, pl.ds(dst, 1)],
            send_sem=esend.at[b, i],
            recv_sem=erecv.at[b, i],
            device_id=(g + 1, to),
            device_id_type=MESH,
        )

    def out_copy(b, k):
        rows = pl.ds(k * cr, cr)
        return pltpu.make_async_copy(
            o_buf.at[b, rows], out.at[0, b, rows], osem.at[b, k]
        )

    span = cr * cols
    width = K2

    def order(p):
        return jnp.where(p == n - 1, n - 1, jnp.where(p == n - 2, 0, p + 1))

    def section(b, p):
        k = order(p)

        @pl.when(g > 0)
        def _():
            @pl.when(p == 0)
            def _():
                for j in range(3):
                    chunk_copy(b, j).wait_recv()

            @pl.when((p > 0) & (p < n - 2))
            def _():
                chunk_copy(b, p + 2).wait_recv()

        @pl.when((p == n - 2) & (s > 0))
        def _():
            edge_copy(b, False).wait_recv()

        @pl.when((p == n - 1) & (s < N - 1))
        def _():
            edge_copy(b, True).wait_recv()

        data = jnp.concatenate(
            [z_buf[b, pl.ds(k * cr + a, cr)].reshape(span, K2) for a in range(3)],
            axis=1,
        )
        place = lax.broadcasted_iota(jnp.int32, (cr, cols, width), 1).reshape(span, width)
        for q in range(K2 // width):
            part = [
                jnp.dot(
                    data,
                    wsec_v[:, c * K2 + q * width : c * K2 + (q + 1) * width],
                    preferred_element_type=jnp.float32,
                )
                for c in range(3)
            ]
            left = jnp.where(place == 0, 0.0, pltpu.roll(part[0], 1, 0))
            right = jnp.where(place == cols - 1, 0.0, pltpu.roll(part[2], span - 1, 0))
            inner = z_buf[
                b, pl.ds(k * cr + 1, cr), :, q * width : (q + 1) * width
            ].reshape(span, width)
            value = jnp.maximum(inner.astype(jnp.float32) + left + part[1] + right, 0.0)
            o_buf[b, pl.ds(k * cr, cr), :, q * width : (q + 1) * width] = value.astype(
                jnp.bfloat16
            ).reshape(cr, cols, width)
        out_copy(b, k).start()

        @pl.when(g < S - 1)
        def _():
            @pl.when((k == 0) & (s > 0))
            def _():
                edge_copy(b, True).start()

            @pl.when((k == n - 1) & (s < N - 1))
            def _():
                edge_copy(b, False).start()

            @pl.when(p >= 2)
            def _():
                chunk_copy(b, order(p - 2)).wait_send()

            if b > 0:

                @pl.when(p < 2)
                def _():
                    chunk_copy(b - 1, order(p + n - 2)).wait_send()

            chunk_copy(b, k).start()

    for b in range(B):

        @pl.when(g == 0)
        def _():
            arrive(b)

        def step(p, carry):
            section(b, p)
            return carry

        lax.fori_loop(0, n, step, 0)

    for b in range(B):
        for i, (dg, ds) in enumerate(DIRS):

            @pl.when(inside(g + dg, s + ds))
            def _():
                border(b, i).wait_send()

        if b == B - 1:
            for away, home, remote, local in pieces(b):

                @pl.when(away)
                def _():
                    remote().wait_send()

        @pl.when((g == 0) & (s > 0))
        def _():
            strip_copy(b, True).wait_send()

        @pl.when((g == 0) & (s < N - 1))
        def _():
            strip_copy(b, False).wait_send()

        @pl.when(g < S - 1)
        def _():
            @pl.when(s > 0)
            def _():
                edge_copy(b, True).wait_send()

            @pl.when(s < N - 1)
            def _():
                edge_copy(b, False).wait_send()

            if b == B - 1:
                chunk_copy(b, 0).wait_send()
                chunk_copy(b, n - 1).wait_send()

        for k in range(n):
            out_copy(b, k).wait()


def shards(S, N, features, weight_first, weight_second, weight_down, section_weights):
    B, R, C, K1 = features.shape
    K2 = weight_down.shape[3]
    RD, CD = R // 2, C // 2
    m = N // S
    sr = RD // m
    cols = CD * N
    n = sr // max(1, 256 // cols)
    pitch = R + EDGE
    bf16, f32 = jnp.bfloat16, jnp.float32
    dma = pltpu.SemaphoreType.DMA
    anywhere = pl.BlockSpec(memory_space=pl.ANY)
    flops = 2 * B * (R * C * 18 * K1 * K1 + RD * CD * 4 * K1 * K2 + sr * cols * 9 * K2 * K2)
    return pl.pallas_call(
        functools.partial(kernel, (S, N, B, R, C, K1, K2)),
        out_shape=jax.ShapeDtypeStruct((1, B, sr, cols, K2), bf16),
        in_specs=[pl.BlockSpec(memory_space=pltpu.HBM)] * 5,
        out_specs=anywhere,
        scratch_shapes=[
            pltpu.VMEM((B, R, C, K1), bf16),
            pltpu.VMEM((B, C + 4, EDGE, K1), bf16),
            pltpu.VMEM((B, C + 4, EDGE, K1), bf16),
            pltpu.VMEM((B, C + 4, pitch, K1), bf16),
            pltpu.VMEM((C + 2, pitch, K1), bf16),
            pltpu.VMEM((K1 // 128, C * R, 128), f32),
            pltpu.VMEM((B, RD * CD, K2), bf16),
            pltpu.VMEM((B, N, sr * CD, K2), bf16),
            pltpu.VMEM((B, sr + 2, cols, K2), bf16),
            pltpu.VMEM((B, sr, cols, K2), bf16),
            pltpu.VMEM((3 * K1, 3 * K1), bf16),
            pltpu.VMEM((3 * K1, 3 * K1), bf16),
            pltpu.VMEM((4 * K1, K2), bf16),
            pltpu.VMEM((3 * K2, 3 * K2), bf16),
            dma((31,)),
            dma((B,)),
            dma((B, 8)),
            dma((B, 8)),
            dma((B, m)),
            dma((B, N)),
            dma((B, n)),
            dma((B, n)),
            dma((B, 2)),
            dma((B, 2)),
            dma((B, 2)),
            dma((B, n)),
        ],
        compiler_params=pltpu.CompilerParams(
            collective_id=0, has_side_effects=True, vmem_limit_bytes=56 * 1024 * 1024
        ),
        cost_estimate=pl.CostEstimate(
            flops=flops, bytes_accessed=16 * 1024 * 1024, transcendentals=0
        ),
    )(
        features,
        weight_first,
        weight_second,
        weight_down,
        section_weights,
    )


def solution(mesh):
    return jax.shard_map(
        functools.partial(shards, mesh.shape["segment"], mesh.shape["strip"]),
        mesh=mesh,
        in_specs=(
            P(None, "segment", "strip", None),
            P(),
            P(),
            P(),
            P("segment", None, None, None, None),
        ),
        out_specs=P("segment", None, "strip", None, None),
        check_vma=False,
    )
```
